512 devices in a mesh: tok: 32 (over x, z), img: 16 (over y, core).
Axes of the slice: x: 4, y: 8, z: 8, core: 2. Of those that a mesh axis runs over, the one named last changes fastest.
Arguments:
- query_in: bfloat16 [2, 16, 4096, 1120], P(None, 'img', 'tok'), may hold values from -6 to 6
- key_in: bfloat16 [2, 16, 4096, 1120], P(None, 'img', 'tok'), may hold values from -6 to 6
- value_in: bfloat16 [2, 16, 4096, 1120], P(None, 'img', 'tok'), may hold values from -6 to 6
- cotangent: bfloat16 [2, 16, 4096, 1152], P(None, 'img', 'tok'), may hold values from -6 to 6
- out_weight: bfloat16 [1120, 1152], P('tok', 'img'), may hold values from -0.1875 to 0.1875
- gate_table: float32 [1152], replicated, may hold values from -6 to 6
- time_gate: float32 [2, 16, 1152], P(None, 'img'), may hold values from -6 to 6
Outputs:
- query_grad: bfloat16 [2, 16, 4096, 1120], P(None, 'img', 'tok')
- key_grad: bfloat16 [2, 16, 4096, 1120], P(None, 'img', 'tok')
- value_grad: bfloat16 [2, 16, 4096, 1120], P(None, 'img', 'tok')
- gate_grad: float32 [1152], P('img')
- weight_grad: float32 [1120, 1152], P('tok', 'img')
The draws below stay inside these ranges and needn't reach their ends.
All inputs are finite; a program needn't handle non-finite values.
Results may differ from the reference program's by a relative error of at most 0.022.
Values may be sent and summed in bfloat16 or wider, within the bound.
A program may use at most 64 MiB of HBM per device.

```python
import jax
import jax.numpy as jnp
from jax import lax

HEADS = 10
HEAD = 112
F = 1120
DW = 1152
STEPS = 2
LOSS_SCALE = 1024
TOK_DEV = 128
TOK_IMG = 4096
IMAGES = 16
N_TOK = 32


def level_of(stream_key, dims, shards, least, top_value):
    factor_of = 1.0
    for dim, shards_of in shards:
        heights = jax.random.uniform(jax.random.fold_in(jax.random.fold_in(stream_key, 6), dim), (shards_of,), jnp.float32, least / len(shards), top_value / len(shards))
        factor_of = factor_of * jnp.repeat(jnp.exp(heights), dims[dim] // shards_of).reshape((-1,) + (1,) * (len(dims) - 1 - dim))
    return factor_of


def centred(own_key, shape, scale, reach, cuts=(), held_as=jnp.bfloat16):
    array = scale * jax.random.normal(own_key, shape, jnp.float32)
    if cuts:
        array = array * level_of(own_key, shape, cuts, -0.22, 0.18)
    return jnp.clip(array, -reach, reach).astype(held_as)


def setup_inputs(seed: int = 0) -> dict:
    arg_keys = jax.random.split(jax.random.key(seed), 8)
    return {
        "query_in": centred(arg_keys[0], (STEPS, IMAGES, TOK_IMG, F), 1.0, 6.0, ((1, 16), (2, 32))),
        "key_in": centred(arg_keys[1], (STEPS, IMAGES, TOK_IMG, F), 1.0, 6.0, ((1, 16), (2, 32))),
        "value_in": centred(arg_keys[2], (STEPS, IMAGES, TOK_IMG, F), 1.0, 6.0, ((1, 16), (2, 32))),
        "cotangent": centred(arg_keys[3], (STEPS, IMAGES, TOK_IMG, DW), 1.0, 6.0, ((1, 16), (2, 32))),
        "out_weight": centred(arg_keys[4], (F, DW), F ** -0.5, 0.1875, ((0, 32), (1, 16))),
        "gate_table": centred(arg_keys[5], (DW,), 1.0, 6.0, (), jnp.float32),
        "time_gate": centred(arg_keys[6], (STEPS, IMAGES, DW), 0.5, 6.0, ((1, 16),), jnp.float32),
    }


def kernel(values_in):
    return jnp.where(values_in > 0, values_in + 1.0, jnp.exp(jnp.minimum(values_in, 0.0)))


def kernel_slope(values_in):
    return jnp.where(values_in > 0, 1.0, jnp.exp(jnp.minimum(values_in, 0.0)))


def one_pair(query_one, key_one, value_one, cotan_one, gate_one, out_weight):
    highest = lax.Precision.HIGHEST
    tok_rows = query_one.shape[0]
    query_f = query_one.astype(jnp.float32).reshape(tok_rows, HEADS, HEAD)
    key_f = key_one.astype(jnp.float32).reshape(tok_rows, HEADS, HEAD)
    value_f = value_one.astype(jnp.float32).reshape(tok_rows, HEADS, HEAD)
    kern_q = kernel(query_f)
    kern_k = kernel(key_f)
    state = jnp.einsum('the,thf->hef', kern_k, value_f, precision=highest)
    key_sum = jnp.sum(kern_k, axis=0)
    numerator = jnp.einsum('the,hef->thf', kern_q, state, precision=highest)
    denominator = jnp.einsum('the,he->th', kern_q, key_sum, precision=highest)
    attn_ratio = numerator / denominator[..., None]
    attended = attn_ratio.astype(jnp.bfloat16).reshape(tok_rows, HEADS * HEAD)
    projected = jnp.dot(attended, out_weight, preferred_element_type=jnp.float32)
    cotan_f = cotan_one.astype(jnp.float32)
    gate_part = jnp.sum(cotan_f * projected, axis=0)
    scaled = (LOSS_SCALE * gate_one[None, :] * cotan_f).astype(jnp.bfloat16)
    d_attended = lax.dot_general(scaled, out_weight, (((1,), (1,)), ((), ())), preferred_element_type=jnp.float32)
    d_attended = d_attended.reshape(tok_rows, HEADS, HEAD)
    d_numer = d_attended / denominator[..., None]
    d_denom = -jnp.sum(d_numer * attn_ratio, axis=-1)
    d_state = jnp.einsum('the,thf->hef', kern_q, d_numer, precision=highest)
    d_keysum = jnp.einsum('the,th->he', kern_q, d_denom, precision=highest)
    d_kernq = jnp.einsum('thf,hef->the', d_numer, state, precision=highest) + d_denom[..., None] * key_sum[None]
    d_kernk = jnp.einsum('thf,hef->the', value_f, d_state, precision=highest) + d_keysum[None]
    d_value = jnp.einsum('the,hef->thf', kern_k, d_state, precision=highest)
    query_grad = (d_kernq * kernel_slope(query_f)).astype(jnp.bfloat16).reshape(tok_rows, HEADS * HEAD)
    key_grad = (d_kernk * kernel_slope(key_f)).astype(jnp.bfloat16).reshape(tok_rows, HEADS * HEAD)
    value_grad = d_value.astype(jnp.bfloat16).reshape(tok_rows, HEADS * HEAD)
    return query_grad, key_grad, value_grad, gate_part, attended, scaled


def reference(query_in, key_in, value_in, cotangent, out_weight, gate_table, time_gate):
    pairs = STEPS * IMAGES
    feat_count = HEADS * HEAD
    query_all = query_in.reshape(pairs, TOK_IMG, feat_count)
    key_all = key_in.reshape(pairs, TOK_IMG, feat_count)
    value_all = value_in.reshape(pairs, TOK_IMG, feat_count)
    cotan_all = cotangent.reshape(pairs, TOK_IMG, DW)
    gate_all = (gate_table[None, None, :] + time_gate).reshape(pairs, DW)

    def single(members):
        return one_pair(members[0], members[1], members[2], members[3], members[4], out_weight)

    query_grad, key_grad, value_grad, gate_parts, attended, scaled = lax.map(single, (query_all, key_all, value_all, cotan_all, gate_all))
    gate_grad = jnp.sum(gate_parts, axis=0)
    attended = attended.reshape(STEPS, IMAGES, TOK_IMG, feat_count)
    scaled = scaled.reshape(STEPS, IMAGES, TOK_IMG, DW)
    zero_index = jnp.zeros((), jnp.int32)

    def add_band(index, total):
        index = jnp.asarray(index).astype(jnp.int32)
        image = (index // N_TOK).astype(jnp.int32)
        band = (index % N_TOK).astype(jnp.int32)
        start = (band * TOK_DEV).astype(jnp.int32)
        att_band = lax.dynamic_slice(attended, (zero_index, image, start, zero_index), (STEPS, 1, TOK_DEV, feat_count))
        sc_band = lax.dynamic_slice(scaled, (zero_index, image, start, zero_index), (STEPS, 1, TOK_DEV, DW))
        att_band = att_band.reshape(STEPS * TOK_DEV, feat_count)
        sc_band = sc_band.reshape(STEPS * TOK_DEV, DW)
        term = lax.dot_general(att_band, sc_band, (((0,), (0,)), ((), ())), preferred_element_type=jnp.float32)
        rounded = lax.optimization_barrier(term.astype(jnp.bfloat16)).astype(jnp.float32)
        return total + rounded

    weight_total = lax.fori_loop(0, IMAGES * N_TOK, add_band, jnp.zeros((feat_count, DW), jnp.float32))
    weight_grad = weight_total / LOSS_SCALE
    shape_out = (STEPS, IMAGES, TOK_IMG, feat_count)
    return query_grad.reshape(shape_out), key_grad.reshape(shape_out), value_grad.reshape(shape_out), gate_grad, weight_grad
```

```python
import jax
import jax.numpy as jnp
from jax import lax
from jax.experimental import pallas as pl
from jax.experimental.pallas import tpu as pltpu
from jax.sharding import PartitionSpec as P

HEADS = 10
HEAD = 112
LOSS_SCALE = 1024.0
TOK = 128
F = 1120
DW = 1152
NX, NZ, NY = 4, 8, 8
NT = NX * NZ
LANES = 128
FP = HEADS * LANES
ROWS_T = 35
ROWS_TP = 48
COLS_I = 72
COLS_IP = 80
NG = 2 * NY
DP = NG * COLS_IP
XR = 288
ZR = 48
BF = jnp.bfloat16
F32 = jnp.float32
MESH = pl.DeviceIdType.MESH
NN = (((1,), (0,)), ((), ()))
NTD = (((1,), (1,)), ((), ()))
TN = (((0,), (0,)), ((), ()))


def dot(a, b, dims):
    return lax.dot_general(a, b, dims, preferred_element_type=F32)


def phi(x):
    return jnp.where(x > 0, x + 1.0, jnp.exp(jnp.minimum(x, 0.0)))


def lane_of(shape):
    return lax.broadcasted_iota(jnp.int32, shape, len(shape) - 1)


def row_of(shape):
    return lax.broadcasted_iota(jnp.int32, shape, len(shape) - 2)


def rounded(x):
    return x.astype(BF).astype(F32)


def split_sum(total):
    lane = lane_of(total.shape)
    whole = total[:, HEAD : HEAD + 1] + total[:, HEAD + 1 : HEAD + 2]
    high = rounded(whole)
    out = jnp.where((lane == HEAD) | (lane == HEAD + 2), high, total)
    return jnp.where(lane == HEAD + 1, whole - high, out)


def same(total):
    return total


def loop(first, last, body):
    def step(idx, carry):
        body(idx)
        return carry

    lax.fori_loop(first, last, step, 0)


def kernel(
    q_ref, k_ref, v_ref, cot_ref, w_ref, table_ref, time_ref,
    dq_ref, dk_ref, dv_ref, wg_ref,
    kq, kk, vs, hot_f, hot_d, scaled, sc_rows, sc_cols, cot_cols,
    w_land, w_t, st, d_st, x_src, x_land, z_src, z_land, z_all,
    d_att, att, dna, core_src, core_land, own_band, y_src, y_land, p_src, p_land,
    w_ss, w_rs, wy_ss, wy_rs, wc_ss, wc_rs, ar_ss, ar_rs, c_ss, c_rs, y_ss, y_rs, p_ss, p_rs,
):
    t = lax.axis_index("tok")
    i = lax.axis_index("img")
    x, z = t // NZ, t % NZ
    y, c = i // 2, i % 2
    sib = (t, y * 2 + (1 - c))

    def plane(d):
        return lax.rem(t + d, NT)

    def along_x(d):
        return lax.rem(x + d, NX)

    def along_z(d):
        return lax.rem(z + d, NZ)

    def along_y(d):
        return lax.rem(y + d, NY)

    def remote(src, dst, ss, rs, dev):
        return pltpu.make_async_remote_copy(
            src_ref=src, dst_ref=dst, send_sem=ss, recv_sem=rs, device_id=dev, device_id_type=MESH
        )

    barrier = pltpu.get_barrier_semaphore()

    def greet(dev):
        pl.semaphore_signal(barrier, inc=1, device_id=dev, device_id_type=MESH)

    loop(1, NT, lambda d: greet((plane(d), i)))
    loop(1, NY, lambda d: greet((t, along_y(d) * 2 + c)))
    greet(sib)

    ones = jnp.where(lane_of((2 * TOK, LANES - HEAD)) < 3, 1.0, 0.0).astype(BF)
    none = jnp.zeros((2 * TOK, LANES - HEAD), BF)
    for h in range(HEADS):
        part = slice(HEAD * h, HEAD * h + HEAD)
        kk[h, :, :HEAD] = phi(k_ref[:, part].astype(F32)).astype(BF)
        kk[h, :, HEAD:] = none
        vs[h, :, :HEAD] = v_ref[:, part]
        vs[h, :, HEAD:] = ones

    tail = jnp.zeros((NX * XR - F, LANES), BF)
    for s in range(2):
        for a in range(2):
            x_src[a, s, F:] = tail

    def state_part(s):
        rows = pl.ds(TOK * s, TOK)

        def one(h):
            acc = dot(kk[h, rows, :], vs[h, rows, :], TN)[:HEAD]
            lane = lane_of(acc.shape)
            x_src[0, s, pl.ds(pl.multiple_of(HEAD * h, 16), HEAD), :] = jnp.where(
                lane == HEAD + 1, acc - rounded(acc), acc
            ).astype(BF)

        loop(0, HEADS, one)

    def rs_x(a, s, d):
        to = along_x(d)
        return remote(
            x_src.at[a, s, pl.ds(pl.multiple_of(XR * to, 16), XR)], x_land.at[a, s, d - 1],
            ar_ss.at[a, s, d - 1], ar_rs.at[a, s, d - 1], (to * NZ + z, i),
        )

    def rs_z(a, s, d):
        to = along_z(d)
        return remote(
            z_src.at[a, s, pl.ds(pl.multiple_of(ZR * to, 16), ZR)], z_land.at[a, s, d - 1],
            ar_ss.at[a, s, 2 + d], ar_rs.at[a, s, 2 + d], (x * NZ + to, i),
        )

    def ag_z(a, s, d):
        mine = z_all.at[a, s, pl.ds(pl.multiple_of(ZR * z, 16), ZR)]
        return remote(
            mine, mine, ar_ss.at[a, s, 9 + d], ar_rs.at[a, s, 9 + d], (x * NZ + along_z(d), i)
        )

    def ag_x(a, s, d):
        whole = d_st if a else st
        return remote(
            z_all.at[a, s, pl.ds(0, XR)], whole.at[s, pl.ds(pl.multiple_of(XR * x, 16), XR)],
            ar_ss.at[a, s, 16 + d], ar_rs.at[a, s, 16 + d], (along_x(d) * NZ + z, i),
        )

    def start_x(a, s):
        loop(1, NX, lambda d: rs_x(a, s, d).start())

    def x_to_z(a, s, fix):
        loop(1, NX, lambda d: rs_x(a, s, d).wait_recv())
        total = x_src[a, s, pl.ds(pl.multiple_of(XR * x, 16), XR), :].astype(F32)
        for d in range(NX - 1):
            total = total + x_land[a, s, d].astype(F32)
        z_src[a, s, :XR] = fix(total).astype(BF)
        z_src[a, s, XR:] = jnp.zeros((NZ * ZR - XR, LANES), BF)
        loop(1, NZ, lambda d: rs_z(a, s, d).start())

    def z_to_all(a, s, fix):
        loop(1, NZ, lambda d: rs_z(a, s, d).wait_recv())
        total = z_src[a, s, pl.ds(pl.multiple_of(ZR * z, 16), ZR), :].astype(F32)
        for d in range(NZ - 1):
            total = total + z_land[a, s, d].astype(F32)
        z_all[a, s, pl.ds(pl.multiple_of(ZR * z, 16), ZR), :] = fix(total).astype(BF)
        loop(1, NZ, lambda d: ag_z(a, s, d).start())

    def all_to_x(a, s):
        loop(1, NZ, lambda d: ag_z(a, s, d).wait_recv())
        loop(1, NX, lambda d: ag_x(a, s, d).start())
        whole = d_st if a else st
        whole[s, pl.ds(pl.multiple_of(XR * x, 16), XR), :] = z_all[a, s, :XR]

    def end_x(a, s):
        loop(1, NX, lambda d: ag_x(a, s, d).wait_recv())

    def w_plane(d):
        return remote(w_ref, w_land.at[t], w_ss.at[d - 1], w_rs.at[d - 1], (plane(d), i))

    def group(g):
        return pl.ds(pl.multiple_of(COLS_IP * g, 16), COLS_IP)

    def w_along_y(d):
        mine = w_t.at[group(y * 2 + c)]
        return remote(mine, mine, wy_ss.at[d - 1], wy_rs.at[d - 1], (t, along_y(d) * 2 + c))

    def w_core(d):
        mine = w_t.at[group(along_y(d) * 2 + c)]
        return remote(mine, mine, wc_ss.at[d], wc_rs.at[d], sib)

    state_part(0)
    pl.semaphore_wait(barrier, NT - 1 + NY - 1 + 1)
    loop(1, NT, lambda d: w_plane(d).start())
    start_x(0, 0)
    state_part(1)
    start_x(0, 1)
    w_land[t] = w_ref[...]

    def hot_rows(b):
        shape = (ROWS_TP, FP)
        j, lane = row_of(shape), lane_of(shape)
        f = ROWS_T * b + j
        head = (ROWS_T * b) // HEAD
        at = f + 16 * head + jnp.where(f >= HEAD * (head + 1), 16, 0)
        at = jnp.where(j < ROWS_T, at, jnp.where(j < ROWS_T + 2, HEAD + j - ROWS_T, -1))
        hot_f[pl.ds(pl.multiple_of(ROWS_TP * b, 16), ROWS_TP), :] = jnp.where(lane == at, 1.0, 0.0).astype(BF)

    loop(0, NT, hot_rows)

    def hot_cols(g):
        shape = (COLS_IP, DW)
        j, lane = row_of(shape), lane_of(shape)
        at = jnp.where(j < COLS_I, COLS_I * g + j, -1)
        hot_d[group(g), :] = jnp.where(lane == at, 1.0, 0.0).astype(BF)

    loop(0, NG, hot_cols)

    for s in range(2):
        rows = slice(TOK * s, TOK * s + TOK)
        gate = table_ref[...] + time_ref[s : s + 1, :]
        scaled[rows, :] = ((LOSS_SCALE * gate) * cot_ref[rows, :].astype(F32)).astype(BF)

    x_to_z(0, 0, split_sum)
    x_to_z(0, 1, split_sum)

    def to_groups(b):
        rows = pl.ds(pl.multiple_of(256 * b, 16), 256)
        hot = hot_d[rows, :]
        sc_cols[rows, :] = dot(hot, scaled[...], NTD).astype(BF)
        cot_cols[rows, :] = dot(hot, cot_ref[...], NTD).astype(BF)

    loop(0, DP // 256, to_groups)
    for b in range(DP // 256):
        cols = slice(256 * b, 256 * b + 256)
        sc_rows[:, cols] = dot(scaled[...], hot_d[cols, :], NTD).astype(BF)

    for h in range(HEADS):
        kq[h, :, :HEAD] = phi(q_ref[:, HEAD * h : HEAD * h + HEAD].astype(F32)).astype(BF)
        kq[h, :, HEAD:] = none

    z_to_all(0, 0, split_sum)
    z_to_all(0, 1, split_sum)

    loop(1, NT, lambda d: w_plane(d).wait_recv())
    for b in range(FP // 256):
        cols = slice(256 * b, 256 * b + 256)
        block = dot(w_land[...].reshape(NT * ROWS_TP, LANES), hot_f[:, cols], TN)
        w_t[group(y * 2 + c), cols] = block[:COLS_IP].astype(BF)
    loop(1, NY, lambda d: w_along_y(d).start())
    w_core(0).start()

    all_to_x(0, 0)
    all_to_x(0, 1)

    for d in (1, 7, 2, 6, 3, 5, 4):
        w_along_y(d).wait_recv()
        w_core(NY - d).start()
    loop(0, NY, lambda d: w_core(d).wait_recv())

    for b in range(FP // 256):
        cols = slice(256 * b, 256 * b + 256)
        d_att[:, cols] = dot(sc_rows[...], w_t[:, cols], NN)

    def middle(s):
        rows = pl.ds(TOK * s, TOK)

        for h in range(HEADS):
            cols = slice(LANES * h, LANES * h + LANES)
            e_rows = slice(HEAD * h, HEAD * h + HEAD)
            kq_h = kq[h, rows, :]
            both = dot(kq_h[:, :HEAD], st[s, e_rows, :], NN)
            inv = 1.0 / (both[:, HEAD : HEAD + 1] + both[:, HEAD + 1 : HEAD + 2])
            lane = lane_of(both.shape)
            ratio = jnp.where(lane < HEAD, both * inv, 0.0)
            att[rows, cols] = ratio.astype(BF)
            d_num = rounded(d_att[rows, cols] * inv)
            d_den = -jnp.sum(d_num * ratio, axis=1, keepdims=True)
            high = rounded(d_den)
            full = jnp.where(lane < HEAD, d_num, jnp.where(lane < HEAD + 2, high, 0.0))
            full = jnp.where(lane == HEAD + 2, d_den - high, full).astype(BF)
            dna[h, rows, :] = full
            acc = dot(kq_h, full, TN)[:HEAD]
            x_src[1, s, e_rows, :] = jnp.where(lane_of(acc.shape) == HEAD + 1, 0.0, acc).astype(BF)

    end_x(0, 0)
    middle(0)
    start_x(1, 0)
    end_x(0, 1)
    middle(1)
    start_x(1, 1)

    def band(g):
        block = dot(sc_cols[group(g), :], att[...], NN)
        plain = dot(cot_cols[group(g), :], att[...], NN)
        gate = jnp.sum(plain * w_t[group(g), :].astype(F32), axis=1, keepdims=True)
        high = rounded(gate)
        lane = lane_of(block.shape)
        return jnp.where(lane == HEAD, high, jnp.where(lane == HEAD + 1, gate - high, block))

    def band_core(d):
        return remote(core_src.at[d], core_land.at[d], c_ss.at[d], c_rs.at[d], sib)

    def band_y(d):
        return remote(y_src.at[d], y_land.at[d - 1], y_ss.at[d - 1], y_rs.at[d - 1], (t, along_y(d) * 2 + c))

    def for_sibling(d):
        core_src[d] = band(along_y(d) * 2 + (1 - c)).astype(BF)
        band_core(d).start()

    loop(0, NY, for_sibling)
    x_to_z(1, 0, same)

    def for_self(d):
        own_band[d] = band(along_y(d) * 2 + c)

    loop(0, NY, for_self)
    x_to_z(1, 1, same)

    def add_halves(total):
        lane = lane_of(total.shape)
        whole = total[:, HEAD : HEAD + 1] + total[:, HEAD + 1 : HEAD + 2]
        high = rounded(whole)
        return jnp.where(lane == HEAD, high, jnp.where(lane == HEAD + 1, whole - high, total))

    def to_y(d):
        band_core(d).wait_recv()
        y_src[d] = add_halves(own_band[d] + core_land[d].astype(F32)).astype(BF)

    for d in (4, 3, 5, 2, 6, 1, 7):
        to_y(d)
        band_y(d).start()
    to_y(0)

    z_to_all(1, 0, same)
    z_to_all(1, 1, same)

    def out_heads(ref, s, heads):
        for h in range(HEADS):
            ref[TOK * s : TOK * s + TOK, HEAD * h : HEAD * h + HEAD] = heads(h)[:, :HEAD].astype(BF)

    def dq_head(s):
        rows = slice(TOK * s, TOK * s + TOK)

        def head(h):
            grad = dot(dna[h, rows, :], st[s, HEAD * h : HEAD * h + HEAD, :], NTD)
            return grad * jnp.minimum(kq[h, rows, :HEAD].astype(F32), 1.0)

        return head

    def dk_head(s):
        rows = slice(TOK * s, TOK * s + TOK)

        def head(h):
            grad = dot(vs[h, rows, :], d_st[s, HEAD * h : HEAD * h + HEAD, :], NTD)
            return grad * jnp.minimum(kk[h, rows, :HEAD].astype(F32), 1.0)

        return head

    def dv_head(s):
        rows = slice(TOK * s, TOK * s + TOK)
        return lambda h: dot(kk[h, rows, :HEAD], d_st[s, HEAD * h : HEAD * h + HEAD, :], NN)

    out_heads(dq_ref, 0, dq_head(0))
    out_heads(dq_ref, 1, dq_head(1))
    all_to_x(1, 0)
    all_to_x(1, 1)

    loop(1, NY, lambda d: band_y(d).wait_recv())
    total = y_src[0].astype(F32)
    for d in range(NY - 1):
        total = total + y_land[d].astype(F32)
    total = add_halves(total).astype(BF)
    total = jnp.concatenate([total, jnp.zeros((LANES - COLS_IP, FP), BF)], axis=0)

    def pieces(b):
        rows = pl.ds(pl.multiple_of(ROWS_TP * 4 * b, 16), ROWS_TP * 4)
        p_src[pl.ds(4 * b, 4)] = dot(hot_f[rows, :], total, NTD).astype(BF).reshape(4, ROWS_TP, LANES)

    loop(0, NT // 4, pieces)

    def p_plane(d):
        return remote(p_src.at[plane(d)], p_land.at[d - 1], p_ss.at[d - 1], p_rs.at[d - 1], (plane(d), i))

    loop(1, NT, lambda d: p_plane(d).start())

    for s in range(2):
        end_x(1, s)
        out_heads(dk_ref, s, dk_head(s))
        out_heads(dv_ref, s, dv_head(s))

    loop(1, NT, lambda d: p_plane(d).wait_recv())
    wg_ref[...] = p_src[t].astype(F32) + jnp.sum(p_land[...].astype(F32), axis=0)

    loop(1, NT, lambda d: w_plane(d).wait_send())
    loop(1, NY, lambda d: w_along_y(d).wait_send())
    loop(0, NY, lambda d: w_core(d).wait_send())
    for a in range(2):
        for s in range(2):
            loop(1, NX, lambda d: rs_x(a, s, d).wait_send())
            loop(1, NZ, lambda d: rs_z(a, s, d).wait_send())
            loop(1, NZ, lambda d: ag_z(a, s, d).wait_send())
            loop(1, NX, lambda d: ag_x(a, s, d).wait_send())
    loop(0, NY, lambda d: band_core(d).wait_send())
    loop(1, NY, lambda d: band_y(d).wait_send())
    loop(1, NT, lambda d: p_plane(d).wait_send())


def on_device(query_in, key_in, value_in, cotangent, out_weight, gate_table, time_gate):
    rows = 2 * TOK
    w_pad = jnp.pad(out_weight, ((0, ROWS_TP - ROWS_T), (0, LANES - COLS_I)))
    dma = pltpu.SemaphoreType.DMA
    vm = pltpu.VMEM
    whole = pl.BlockSpec(memory_space=pltpu.VMEM)
    out = pl.pallas_call(
        kernel,
        name="linear_attention_backward",
        out_shape=[jax.ShapeDtypeStruct((rows, F), BF)] * 3 + [jax.ShapeDtypeStruct((ROWS_TP, LANES), F32)],
        in_specs=[whole] * 7,
        out_specs=[whole] * 4,
        scratch_shapes=[
            vm((HEADS, rows, LANES), BF),
            vm((HEADS, rows, LANES), BF),
            vm((HEADS, rows, LANES), BF),
            vm((NT * ROWS_TP, FP), BF),
            vm((DP, DW), BF),
            vm((rows, DW), BF),
            vm((rows, DP), BF),
            vm((DP, rows), BF),
            vm((DP, rows), BF),
            vm((NT, ROWS_TP, LANES), BF),
            vm((DP, FP), BF),
            vm((2, NX * XR, LANES), BF),
            vm((2, NX * XR, LANES), BF),
            vm((2, 2, NX * XR, LANES), BF),
            vm((2, 2, NX - 1, XR, LANES), BF),
            vm((2, 2, NZ * ZR, LANES), BF),
            vm((2, 2, NZ - 1, ZR, LANES), BF),
            vm((2, 2, NZ * ZR, LANES), BF),
            vm((rows, FP), F32),
            vm((rows, FP), BF),
            vm((HEADS, rows, LANES), BF),
            vm((NY, COLS_IP, FP), BF),
            vm((NY, COLS_IP, FP), BF),
            vm((NY, COLS_IP, FP), F32),
            vm((NY, COLS_IP, FP), BF),
            vm((NY - 1, COLS_IP, FP), BF),
            vm((NT, ROWS_TP, LANES), BF),
            vm((NT - 1, ROWS_TP, LANES), BF),
            dma((NT - 1,)), dma((NT - 1,)),
            dma((NY - 1,)), dma((NY - 1,)),
            dma((NY,)), dma((NY,)),
            dma((2, 2, 20)), dma((2, 2, 20)),
            dma((NY,)), dma((NY,)),
            dma((NY - 1,)), dma((NY - 1,)),
            dma((NT - 1,)), dma((NT - 1,)),
        ],
        compiler_params=pltpu.CompilerParams(
            collective_id=0, has_side_effects=True, vmem_limit_bytes=56 * 2**20
        ),
    )(
        query_in.reshape(rows, F),
        key_in.reshape(rows, F),
        value_in.reshape(rows, F),
        cotangent.reshape(rows, DW),
        w_pad,
        gate_table.reshape(1, DW),
        time_gate.reshape(2, DW),
    )
    shape = query_in.shape
    share = out[3]
    return (
        out[0].reshape(shape),
        out[1].reshape(shape),
        out[2].reshape(shape),
        share[ROWS_T, :COLS_I] + share[ROWS_T + 1, :COLS_I],
        share[:ROWS_T, :COLS_I] / LOSS_SCALE,
    )


def solution(mesh):
    big = P(None, "img", "tok", None)
    return jax.shard_map(
        on_device,
        mesh=mesh,
        in_specs=(big, big, big, big, P("tok", "img"), P(), P(None, "img", None)),
        out_specs=(big, big, big, P("img"), P("tok", "img")),
        check_vma=False,
    )
```

```python
import jax
import jax.numpy as jnp
from jax import lax
from jax.experimental import pallas as pl
from jax.experimental.pallas import tpu as pltpu
from jax.sharding import PartitionSpec as P

HEADS = 10
HEAD = 112
LOSS_SCALE = 1024.0
TOK = 128
F = 1120
DW = 1152
NX, NZ, NY = 4, 8, 8
NT = NX * NZ
LANES = 128
FP = 1152
ROWS_T = 35
ROWS_TP = 48
COLS_I = 72
COLS_IP = 80
HALF = NY * COLS_IP
DP = 2 * HALF
XR = 288
ZR = 48
PART = 48
BF = jnp.bfloat16
F32 = jnp.float32
MESH = pl.DeviceIdType.MESH
NN = (((1,), (0,)), ((), ()))
NTD = (((1,), (1,)), ((), ()))
TN = (((0,), (0,)), ((), ()))


def dot(a, b, dims):
    return lax.dot_general(a, b, dims, preferred_element_type=F32)


def phi(x):
    return jnp.where(x > 0, x + 1.0, jnp.exp(jnp.minimum(x, 0.0)))


def lane_of(shape):
    return lax.broadcasted_iota(jnp.int32, shape, len(shape) - 1)


def row_of(shape):
    return lax.broadcasted_iota(jnp.int32, shape, len(shape) - 2)


def rounded(x):
    return x.astype(BF).astype(F32)


def split_sum(total):
    lane = lane_of(total.shape)
    whole = total[:, HEAD : HEAD + 1] + total[:, HEAD + 1 : HEAD + 2]
    high = rounded(whole)
    out = jnp.where((lane == HEAD) | (lane == HEAD + 2), high, total)
    return jnp.where(lane == HEAD + 1, whole - high, out)


def same(total):
    return total


def loop(first, last, body):
    def step(idx, carry):
        body(idx)
        return carry

    lax.fori_loop(first, last, step, 0)


def kernel(
    q_in, k_in, v_in, cot_in, w_ref, table_ref, time_ref,
    dq_ref, dk_ref, dv_ref, wg_ref, gate_ref,
    kq, kk, vs, hot_f, hot_d, scaled, sc_cols, cot_cols,
    w_mine, w_land, w_t, st, d_st, x_src, x_land, z_src, z_land, z_all,
    d_att, att, inv, dna, core_src, core_land, own_band, y_src, y_land, y_mid, y_far, p_src, p_land,
    g_core, g_core_land, g_src, g_land, cot_ref, q_ref, k_ref, v_ref,
    w_ss, w_rs, wy_ss, wy_rs, wc_ss, wc_rs, ar_ss, ar_rs, c_ss, c_rs, y_ss, y_rs, p_ss, p_rs, g_ss, g_rs, in_sem,
):
    t = lax.axis_index("tok")
    i = lax.axis_index("img")
    x, z = t // NZ, t % NZ
    y, c = i // 2, i % 2
    sib = (t, y * 2 + (1 - c))
    sends, recvs = [], {}

    def plane(d):
        return lax.rem(t + d, NT)

    def along_x(d):
        return lax.rem(x + d, NX)

    def along_z(d):
        return lax.rem(z + d, NZ)

    def along_y(d):
        return lax.rem(y + d, NY)

    def remote(src, dst, ss, rs, dev):
        return pltpu.make_async_remote_copy(
            src_ref=src, dst_ref=dst, send_sem=ss, recv_sem=rs, device_id=dev, device_id_type=MESH
        )

    def launch(make, first, last, key):
        loop(first, last, lambda d: make(d).start())
        sends.append((make, first, last))
        recvs[key] = (make, first, last)

    def arrive(key):
        make, first, last = recvs.pop(key)
        loop(first, last, lambda d: make(d).wait_recv())

    def drain():
        for key in list(recvs):
            arrive(key)
        for make, first, last in sends:
            loop(first, last, lambda d: make(d).wait_send())

    barrier = pltpu.get_barrier_semaphore()

    def greet(dev):
        pl.semaphore_signal(barrier, inc=1, device_id=dev, device_id_type=MESH)

    loads = [
        pltpu.make_async_copy(src, dst, in_sem.at[n])
        for n, (src, dst) in enumerate(((k_in, k_ref), (v_in, v_ref), (cot_in, cot_ref), (q_in, q_ref)))
    ]
    for load in loads:
        load.start()
    loop(1, NT, lambda d: greet((plane(d), i)))
    loop(1, NY, lambda d: greet((t, along_y(d) * 2 + c)))
    greet(sib)

    def group(g):
        return pl.ds(pl.multiple_of(COLS_IP * g, 16), COLS_IP)

    def head_rows(h):
        return pl.ds(pl.multiple_of(HEAD * h, 16), HEAD)

    w_mine[...] = jnp.zeros((ROWS_TP, LANES), BF)
    w_mine[:ROWS_T, :COLS_I] = w_ref[...]
    ones = jnp.where(row_of((LANES - HEAD, TOK)) < 3, 1.0, 0.0).astype(BF)

    def state_part(s):
        for h in range(HEADS):
            rows = slice(HEAD * h, HEAD * h + HEAD)
            keys = phi(k_ref[s, rows, :].astype(F32)).astype(BF)
            kk[s, rows, :] = keys
            vs[s, h, :HEAD, :] = v_ref[s, rows, :]
            vs[s, h, HEAD:, :] = ones
            acc = dot(keys, vs[s, h], NTD)
            x_src[0, s, rows, :] = jnp.where(
                lane_of(acc.shape) == HEAD + 1, acc - rounded(acc), acc
            ).astype(BF)

    def rs_x(a, s):
        def make(d):
            to = along_x(d)
            return remote(
                x_src.at[a, s, pl.ds(pl.multiple_of(XR * to, 16), XR)], x_land.at[a, s, d - 1],
                ar_ss.at[a, s, d - 1], ar_rs.at[a, s, d - 1], (to * NZ + z, i),
            )

        return make

    def rs_z(a, s):
        def make(d):
            to = along_z(d)
            return remote(
                z_src.at[a, s, pl.ds(pl.multiple_of(ZR * to, 16), ZR)], z_land.at[a, s, d - 1],
                ar_ss.at[a, s, 2 + d], ar_rs.at[a, s, 2 + d], (x * NZ + to, i),
            )

        return make

    def ag_z(a, s):
        def make(d):
            mine = z_all.at[a, s, pl.ds(pl.multiple_of(ZR * z, 16), ZR)]
            return remote(
                mine, mine, ar_ss.at[a, s, 9 + d], ar_rs.at[a, s, 9 + d], (x * NZ + along_z(d), i)
            )

        return make

    def ag_x(a, s):
        whole = d_st if a else st

        def make(d):
            return remote(
                z_all.at[a, s, pl.ds(0, XR)], whole.at[s, pl.ds(pl.multiple_of(XR * x, 16), XR)],
                ar_ss.at[a, s, 16 + d], ar_rs.at[a, s, 16 + d], (along_x(d) * NZ + z, i),
            )

        return make

    def start_x(a, s):
        launch(rs_x(a, s), 1, NX, ("rx", a, s))

    def x_to_z(a, s, fix):
        arrive(("rx", a, s))
        total = x_src[a, s, pl.ds(pl.multiple_of(XR * x, 16), XR), :].astype(F32)
        for d in range(NX - 1):
            total = total + x_land[a, s, d].astype(F32)
        z_src[a, s, :XR] = fix(total).astype(BF)
        launch(rs_z(a, s), 1, NZ, ("rz", a, s))

    def z_to_all(a, s, fix):
        arrive(("rz", a, s))
        total = z_src[a, s, pl.ds(pl.multiple_of(ZR * z, 16), ZR), :].astype(F32)
        for d in range(NZ - 1):
            total = total + z_land[a, s, d].astype(F32)
        z_all[a, s, pl.ds(pl.multiple_of(ZR * z, 16), ZR), :] = fix(total).astype(BF)
        launch(ag_z(a, s), 1, NZ, ("az", a, s))

    def all_to_x(a, s):
        arrive(("az", a, s))
        launch(ag_x(a, s), 1, NX, ("ax", a, s))
        whole = d_st if a else st
        whole[s, pl.ds(pl.multiple_of(XR * x, 16), XR), :] = z_all[a, s, :XR]

    def w_plane(d):
        return remote(w_mine, w_land.at[t], w_ss.at[d - 1], w_rs.at[d - 1], (plane(d), i))

    def tree(which):
        def make(ss, rs, src, dst, step):
            return remote(src, dst, ss.at[which], rs.at[which], (t, along_y(step) * 2 + c))

        return make

    def w_rows(away, first=0, count=COLS_IP):
        return w_t.at[pl.ds(pl.multiple_of(COLS_IP * (c * NY + along_y(away)) + first, 16), count)]

    def w_near(which):
        part = w_rows(0)
        return tree(which)(wy_ss, wy_rs, part, part, (1, 7, 2, 6)[which])

    def w_far(which):
        part = w_rows((6, 2)[which])
        return tree(4 + which)(wy_ss, wy_rs, part, part, (1, 7)[which])

    def w_half(which):
        part = (w_rows(6, PART, COLS_IP - PART), w_rows(2, 0, PART))[which]
        return tree(6 + which)(wy_ss, wy_rs, part, part, (2, 6)[which])

    def w_core(d):
        mine = w_t.at[group(c * NY + along_y(d))]
        return remote(mine, mine, wc_ss.at[d], wc_rs.at[d], sib)

    def band_core(d):
        return remote(core_src.at[d], core_land.at[d], c_ss.at[d], c_rs.at[d], sib)

    def b_tree(n):
        ahead, behind = along_y(4), along_y(4)
        src, dst, step = (
            lambda: (y_src.at[along_y(1)], y_land.at[0], 1),
            lambda: (y_src.at[along_y(7)], y_land.at[1], 7),
            lambda: (y_mid.at[0], y_land.at[2], 2),
            lambda: (y_mid.at[1], y_land.at[3], 6),
            lambda: (y_src.at[along_y(3)], y_far.at[0], 1),
            lambda: (y_src.at[along_y(5)], y_far.at[1], 7),
            lambda: (y_src.at[ahead, pl.ds(0, PART)], y_far.at[2, pl.ds(0, PART)], 2),
            lambda: (y_src.at[behind, pl.ds(PART, COLS_IP - PART)], y_far.at[2, pl.ds(PART, COLS_IP - PART)], 6),
        )[n]()
        return tree(n)(y_ss, y_rs, src, dst, step)

    def gate_core():
        return remote(g_core, g_core_land, g_ss.at[0], g_rs.at[0], sib)

    def gate_y(d):
        return remote(g_src.at[group(along_y(d))], g_land.at[d - 1], g_ss.at[d], g_rs.at[d], (t, along_y(d) * 2 + c))

    def halves(column):
        high = rounded(column)
        lane = lane_of((column.shape[0], LANES)) + (FP - LANES)
        return jnp.where(lane == F, high, jnp.where(lane == F + 1, column - high, 0.0))

    def add_halves(tile):
        at = F - FP + LANES
        return halves(tile[:, at : at + 1] + tile[:, at + 1 : at + 2])

    def main():
        for a in range(2):
            for s in range(2):
                x_src[a, s, F:] = jnp.zeros((NX * XR - F, LANES), BF)
                z_src[a, s, XR:] = jnp.zeros((NZ * ZR - XR, LANES), BF)
        att[F:, :] = jnp.zeros((FP - F, 2 * TOK), BF)
        pl.semaphore_wait(barrier, NT - 1 + NY - 1 + 1)
        launch(w_plane, 1, NT, "w")
        loads[0].wait()
        loads[1].wait()
        state_part(0)
        start_x(0, 0)
        state_part(1)
        start_x(0, 1)
        w_land[t] = w_mine[...]

        def hot_rows(b):
            shape = (ROWS_TP, FP)
            j, lane = row_of(shape), lane_of(shape)
            at = jnp.where(j < ROWS_T, ROWS_T * b + j, jnp.where(j < ROWS_T + 2, F - ROWS_T + j, -1))
            hot_f[pl.ds(pl.multiple_of(ROWS_TP * b, 16), ROWS_TP), :] = jnp.where(lane == at, 1.0, 0.0).astype(BF)

        loop(0, NT, hot_rows)
        x_to_z(0, 0, split_sum)
        x_to_z(0, 1, split_sum)

        def hot_cols(g):
            shape = (COLS_IP, DW)
            j, lane = row_of(shape), lane_of(shape)
            first = COLS_I * (2 * (g % NY) + g // NY)
            hot_d[group(g), :] = jnp.where(lane == jnp.where(j < COLS_I, first + j, -1), 1.0, 0.0).astype(BF)

        loop(0, 2 * NY, hot_cols)
        loads[2].wait()
        loads[3].wait()
        for s in range(2):
            rows = slice(TOK * s, TOK * s + TOK)
            gate = table_ref[...].reshape(1, DW) + time_ref[s]
            scaled[rows, :] = ((LOSS_SCALE * gate) * cot_ref[rows, :].astype(F32)).astype(BF)

        def to_groups(b):
            rows = pl.ds(pl.multiple_of(256 * b, 16), 256)
            hot = hot_d[rows, :]
            sc_cols[rows, :] = dot(hot, scaled[...], NTD).astype(BF)
            cot_cols[rows, :] = dot(hot, cot_ref[...], NTD).astype(BF)

        loop(0, DP // 256, to_groups)
        for s in range(2):
            for h in range(HEADS):
                rows = slice(HEAD * h, HEAD * h + HEAD)
                kq[s, rows, :] = phi(q_ref[s, rows, :].astype(F32)).astype(BF)

        z_to_all(0, 0, split_sum)
        z_to_all(0, 1, split_sum)

        arrive("w")
        for b in range(FP // 384):
            cols = slice(384 * b, 384 * b + 384)
            block = dot(w_land[...].reshape(NT * ROWS_TP, LANES), hot_f[:, cols], TN)
            w_t[group(c * NY + y), cols] = block[:COLS_IP].astype(BF)
        for n in range(4):
            w_near(n).start()
        w_core(0).start()

        all_to_x(0, 0)
        all_to_x(0, 1)

        def ratios(s):
            cols = slice(TOK * s, TOK * s + TOK)
            for h in range(HEADS):
                rows = slice(HEAD * h, HEAD * h + HEAD)
                both = dot(st[s, rows, :], kq[s, rows, :], TN)
                one_over = 1.0 / (both[HEAD : HEAD + 1] + both[HEAD + 1 : HEAD + 2])
                inv[s, h] = one_over
                att[rows, cols] = (both[:HEAD] * one_over).astype(BF)

        arrive(("ax", 0, 0))
        ratios(0)
        w_near(2).wait_recv()
        w_far(0).start()
        w_half(0).start()
        w_core(6).start()
        w_near(3).wait_recv()
        w_far(1).start()
        w_half(1).start()
        w_core(2).start()
        w_near(0).wait_recv()
        w_core(7).start()
        w_near(1).wait_recv()
        w_core(1).start()
        arrive(("ax", 0, 1))
        ratios(1)

        def band(first):
            rows = pl.ds(pl.multiple_of(first, 16), 2 * COLS_IP)
            return dot(sc_cols[rows, :], att[...], NTD)

        for b in range(NY // 2):
            block = band(HALF * (1 - c) + 2 * COLS_IP * b)
            for e in range(2):
                core_src[2 * b + e] = block[COLS_IP * e : COLS_IP * (e + 1)].astype(BF)
            loop(2 * b, 2 * b + 2, lambda d: band_core(d).start())
        for b in range(NY // 2):
            block = band(HALF * c + 2 * COLS_IP * b)
            for e in range(2):
                own_band[2 * b + e] = block[COLS_IP * e : COLS_IP * (e + 1)]
        loop(0, NY, lambda d: band_core(d).wait_recv())

        def to_y(d):
            y_src[d] = (own_band[d] + core_land[d].astype(F32)).astype(BF)

        loop(0, NY, to_y)
        for n in (4, 5, 6, 7, 0, 1):
            b_tree(n).start()
        w_far(0).wait_recv()
        w_core(5).start()
        w_far(1).wait_recv()
        w_core(3).start()
        w_half(0).wait_recv()
        w_half(1).wait_recv()
        w_core(4).start()
        loop(0, NY, lambda d: w_core(d).wait_recv())

        for b in range(FP // 384):
            cols = slice(384 * b, 384 * b + 384)
            d_att[cols, :] = dot(w_t[:, cols], sc_cols[...], TN)

        def middle(s):
            cols = slice(TOK * s, TOK * s + TOK)
            for h in range(HEADS):
                rows = slice(HEAD * h, HEAD * h + HEAD)
                d_num = rounded(d_att[rows, cols] * inv[s, h])
                d_den = -jnp.sum(d_num * att[rows, cols].astype(F32), axis=0, keepdims=True)
                high = rounded(d_den)
                row = row_of((LANES - HEAD, TOK))
                rest = jnp.where(row < 2, high, jnp.where(row == 2, d_den - high, 0.0))
                dna[s, h, :HEAD] = d_num.astype(BF)
                dna[s, h, HEAD:] = rest.astype(BF)
                acc = dot(kq[s, rows, :], dna[s, h], NTD)
                x_src[1, s, rows, :] = jnp.where(lane_of(acc.shape) == HEAD + 1, 0.0, acc).astype(BF)

        middle(0)
        start_x(1, 0)
        middle(1)
        start_x(1, 1)

        def gate_tile(first):
            rows = pl.ds(pl.multiple_of(first, 16), HALF // 2)
            part = dot(w_t[rows, :], att[...], NN) * cot_cols[rows, :].astype(F32)
            return halves(jnp.sum(part, axis=1, keepdims=True))

        for b in range(2):
            rows = slice(HALF // 2 * b, HALF // 2 * (b + 1))
            g_core[rows, :] = gate_tile(HALF * (1 - c) + HALF // 2 * b).astype(BF)
        gate_core().start()
        x_to_z(1, 0, same)
        x_to_z(1, 1, same)
        gate_core().wait_recv()
        for b in range(2):
            rows = slice(HALF // 2 * b, HALF // 2 * (b + 1))
            part = gate_tile(HALF * c + HALF // 2 * b) + g_core_land[rows, :].astype(F32)
            g_src[rows, :] = add_halves(part).astype(BF)
        launch(gate_y, 1, NY, "g")

        b_tree(4).wait_recv()
        b_tree(6).wait_recv()
        to = along_y(2)
        y_mid[0] = (y_src[to].astype(F32) + y_far[0].astype(F32)).astype(BF)
        y_mid[0, :PART] = (
            y_src[to, :PART].astype(F32) + y_far[0, :PART].astype(F32) + y_far[2, :PART].astype(F32)
        ).astype(BF)
        b_tree(2).start()
        b_tree(5).wait_recv()
        b_tree(7).wait_recv()
        to = along_y(6)
        y_mid[1] = (y_src[to].astype(F32) + y_far[1].astype(F32)).astype(BF)
        y_mid[1, PART:] = (
            y_src[to, PART:].astype(F32) + y_far[1, PART:].astype(F32) + y_far[2, PART:].astype(F32)
        ).astype(BF)
        b_tree(3).start()

        z_to_all(1, 0, same)
        z_to_all(1, 1, same)

        for s in range(2):
            for h in range(HEADS):
                rows = slice(HEAD * h, HEAD * h + HEAD)
                grad = dot(st[s, rows, :], dna[s, h], NN)
                slope = jnp.minimum(kq[s, rows, :].astype(F32), 1.0)
                dq_ref[s, rows, :] = (grad * slope).astype(BF)
        all_to_x(1, 0)
        all_to_x(1, 1)

        def last_grads(s):
            arrive(("ax", 1, s))
            for h in range(HEADS):
                rows = slice(HEAD * h, HEAD * h + HEAD)
                keys = kk[s, rows, :]
                state = d_st[s, rows, :]
                grad = dot(state, vs[s, h], NN)
                dk_ref[s, rows, :] = (grad * jnp.minimum(keys.astype(F32), 1.0)).astype(BF)
                dv_ref[s, rows, :] = dot(state, keys, TN)[:HEAD].astype(BF)

        last_grads(0)
        last_grads(1)

        for n in range(4):
            b_tree(n).wait_recv()
        total = y_src[y].astype(F32)
        for d in range(4):
            total = total + y_land[d].astype(F32)
        arrive("g")
        gate = g_src[group(y), :].astype(F32)
        for d in range(NY - 1):
            gate = gate + g_land[d].astype(F32)
        last = total[:, FP - LANES :] + add_halves(gate)
        total = jnp.concatenate([total[:, : FP - LANES], last], axis=1).astype(BF)
        total = jnp.concatenate([total, jnp.zeros((LANES - COLS_IP, FP), BF)], axis=0)

        def pieces(b):
            rows = pl.ds(pl.multiple_of(ROWS_TP * 8 * b, 16), ROWS_TP * 8)
            p_src[pl.ds(8 * b, 8)] = dot(hot_f[rows, :], total, NTD).astype(BF).reshape(8, ROWS_TP, LANES)

        loop(0, NT // 8, pieces)

        def p_plane(d):
            return remote(p_src.at[plane(d)], p_land.at[d - 1], p_ss.at[d - 1], p_rs.at[d - 1], (plane(d), i))

        launch(p_plane, 1, NT, "p")
        arrive("p")
        total = p_src[t].astype(F32)
        for d in range(NT - 1):
            total = total + p_land[d].astype(F32)
        wg_ref[...] = total[:ROWS_T, :COLS_I] * (1.0 / LOSS_SCALE)
        gate_ref[...] = total[ROWS_T : ROWS_T + 1, :COLS_I] + total[ROWS_T + 1 : ROWS_T + 2, :COLS_I]

    main()
    drain()
    for n in range(4):
        w_near(n).wait_send()
    for n in range(2):
        w_far(n).wait_send()
        w_half(n).wait_send()
    loop(0, NY, lambda d: w_core(d).wait_send())
    loop(0, NY, lambda d: band_core(d).wait_send())
    for n in range(8):
        b_tree(n).wait_send()
    gate_core().wait_send()


def on_device(query_in, key_in, value_in, cotangent, out_weight, gate_table, time_gate):
    dma = pltpu.SemaphoreType.DMA
    vm = pltpu.VMEM
    whole = pl.BlockSpec(memory_space=pltpu.VMEM)
    turned = lambda a: jnp.swapaxes(a, 2, 3).reshape(2, F, TOK)
    out = pl.pallas_call(
        kernel,
        name="linear_attention_backward",
        out_shape=[jax.ShapeDtypeStruct((2, F, TOK), BF)] * 3
        + [jax.ShapeDtypeStruct((ROWS_T, COLS_I), F32), jax.ShapeDtypeStruct((1, COLS_I), F32)],
        in_specs=[pl.BlockSpec(memory_space=pl.ANY)] * 4 + [whole] * 3,
        out_specs=[whole] * 5,
        scratch_shapes=[
            vm((2, F, TOK), BF),
            vm((2, F, TOK), BF),
            vm((2, HEADS, LANES, TOK), BF),
            vm((NT * ROWS_TP, FP), BF),
            vm((DP, DW), BF),
            vm((2 * TOK, DW), BF),
            vm((DP, 2 * TOK), BF),
            vm((DP, 2 * TOK), BF),
            vm((ROWS_TP, LANES), BF),
            vm((NT, ROWS_TP, LANES), BF),
            vm((DP, FP), BF),
            vm((2, NX * XR, LANES), BF),
            vm((2, NX * XR, LANES), BF),
            vm((2, 2, NX * XR, LANES), BF),
            vm((2, 2, NX - 1, XR, LANES), BF),
            vm((2, 2, NZ * ZR, LANES), BF),
            vm((2, 2, NZ - 1, ZR, LANES), BF),
            vm((2, 2, NZ * ZR, LANES), BF),
            vm((FP, 2 * TOK), F32),
            vm((FP, 2 * TOK), BF),
            vm((2, HEADS, 1, TOK), F32),
            vm((2, HEADS, LANES, TOK), BF),
            vm((NY, COLS_IP, FP), BF),
            vm((NY, COLS_IP, FP), BF),
            vm((NY, COLS_IP, FP), F32),
            vm((NY, COLS_IP, FP), BF),
            vm((4, COLS_IP, FP), BF),
            vm((2, COLS_IP, FP), BF),
            vm((3, COLS_IP, FP), BF),
            vm((NT, ROWS_TP, LANES), BF),
            vm((NT - 1, ROWS_TP, LANES), BF),
            vm((HALF, LANES), BF),
            vm((HALF, LANES), BF),
            vm((HALF, LANES), BF),
            vm((NY - 1, COLS_IP, LANES), BF),
            vm((2 * TOK, DW), BF),
            vm((2, F, TOK), BF),
            vm((2, F, TOK), BF),
            vm((2, F, TOK), BF),
            dma((NT - 1,)), dma((NT - 1,)),
            dma((8,)), dma((8,)),
            dma((NY,)), dma((NY,)),
            dma((2, 2, 20)), dma((2, 2, 20)),
            dma((NY,)), dma((NY,)),
            dma((8,)), dma((8,)),
            dma((NT - 1,)), dma((NT - 1,)),
            dma((NY,)), dma((NY,)), dma((4,)),
        ],
        compiler_params=pltpu.CompilerParams(
            collective_id=0, has_side_effects=True, vmem_limit_bytes=56 * 2**20
        ),
    )(
        turned(query_in),
        turned(key_in),
        turned(value_in),
        cotangent.reshape(2 * TOK, DW),
        out_weight,
        gate_table,
        time_gate,
    )
    back = lambda a: jnp.swapaxes(a.reshape(2, 1, F, TOK), 2, 3)
    return back(out[0]), back(out[1]), back(out[2]), out[4].reshape(COLS_I), out[3]


def solution(mesh):
    big = P(None, "img", "tok", None)
    return jax.shard_map(
        on_device,
        mesh=mesh,
        in_specs=(big, big, big, big, P("tok", "img"), P(), P(None, "img", None)),
        out_specs=(big, big, big, P("img"), P("tok", "img")),
        check_vma=False,
    )
```

```python
import jax
import jax.numpy as jnp
from jax import lax
from jax.experimental import pallas as pl
from jax.experimental.pallas import tpu as pltpu
from jax.sharding import PartitionSpec as P

HEADS = 10
HEAD = 112
LOSS_SCALE = 1024.0
TOK = 128
F = 1120
DW = 1152
NX, NZ, NY = 4, 8, 8
NT = NX * NZ
LANES = 128
FP = 1152
ROWS_T = 35
ROWS_TP = 48
COLS_I = 72
COLS_IP = 80
HALF = NY * COLS_IP
DP = 2 * HALF
XR = 288
ZR = 48
PART = 48
BF = jnp.bfloat16
F32 = jnp.float32
MESH = pl.DeviceIdType.MESH
NN = (((1,), (0,)), ((), ()))
NTD = (((1,), (1,)), ((), ()))
TN = (((0,), (0,)), ((), ()))


def dot(a, b, dims):
    return lax.dot_general(a, b, dims, preferred_element_type=F32)


def phi(x):
    return jnp.where(x > 0, x + 1.0, jnp.exp(jnp.minimum(x, 0.0)))


def lane_of(shape):
    return lax.broadcasted_iota(jnp.int32, shape, len(shape) - 1)


def row_of(shape):
    return lax.broadcasted_iota(jnp.int32, shape, len(shape) - 2)


def rounded(x):
    return x.astype(BF).astype(F32)


def split_sum(total):
    lane = lane_of(total.shape)
    whole = total[:, HEAD : HEAD + 1] + total[:, HEAD + 1 : HEAD + 2]
    high = rounded(whole)
    out = jnp.where((lane == HEAD) | (lane == HEAD + 2), high, total)
    return jnp.where(lane == HEAD + 1, whole - high, out)


def same(total):
    return total


def loop(first, last, body):
    def step(idx, carry):
        body(idx)
        return carry

    lax.fori_loop(first, last, step, 0)


def kernel(
    q_in, k_in, v_in, cot_in, w_ref, table_ref, time_ref,
    dq_ref, dk_ref, dv_ref, wg_ref, gate_ref,
    kq, kk, vs, hot_f, hot_d, scaled, sc_cols, cot_cols,
    w_mine, w_land, w_t, st, d_st, x_src, x_land, z_src, z_land, z_all,
    d_att, att, inv, dna, core_src, core_land, own_band, y_src, y_land, y_mid, y_far, p_sum, p_src, p_land,
    g_core, g_core_land, g_src, g_land, cot_ref, q_ref, k_ref, v_ref,
    w_ss, w_rs, wy_ss, wy_rs, wc_ss, wc_rs, ar_ss, ar_rs, c_ss, c_rs, y_ss, y_rs, p_ss, p_rs, g_ss, g_rs, in_sem,
):
    t = lax.axis_index("tok")
    i = lax.axis_index("img")
    x, z = t // NZ, t % NZ
    y, c = i // 2, i % 2
    sib = (t, y * 2 + (1 - c))
    sends, recvs = [], {}

    def plane(d):
        return lax.rem(t + d, NT)

    def along_x(d):
        return lax.rem(x + d, NX)

    def along_z(d):
        return lax.rem(z + d, NZ)

    def along_y(d):
        return lax.rem(y + d, NY)

    def remote(src, dst, ss, rs, dev):
        return pltpu.make_async_remote_copy(
            src_ref=src, dst_ref=dst, send_sem=ss, recv_sem=rs, device_id=dev, device_id_type=MESH
        )

    def launch(make, first, last, key):
        loop(first, last, lambda d: make(d).start())
        sends.append((make, first, last))
        recvs[key] = (make, first, last)

    def arrive(key):
        make, first, last = recvs.pop(key)
        loop(first, last, lambda d: make(d).wait_recv())

    def drain():
        for key in list(recvs):
            arrive(key)
        for make, first, last in sends:
            loop(first, last, lambda d: make(d).wait_send())

    barrier = pltpu.get_barrier_semaphore()

    def greet(dev):
        pl.semaphore_signal(barrier, inc=1, device_id=dev, device_id_type=MESH)

    loads = [
        pltpu.make_async_copy(src, dst, in_sem.at[n])
        for n, (src, dst) in enumerate(((k_in, k_ref), (v_in, v_ref), (cot_in, cot_ref), (q_in, q_ref)))
    ]
    for load in loads:
        load.start()
    loop(1, NT, lambda d: greet((plane(d), i)))
    loop(1, NY, lambda d: greet((t, along_y(d) * 2 + c)))
    greet(sib)

    def group(g):
        return pl.ds(pl.multiple_of(COLS_IP * g, 16), COLS_IP)

    def head_rows(h):
        return pl.ds(pl.multiple_of(HEAD * h, 16), HEAD)

    w_mine[...] = jnp.zeros((ROWS_TP, LANES), BF)
    w_mine[:ROWS_T, :COLS_I] = w_ref[...]
    ones = jnp.where(row_of((LANES - HEAD, TOK)) < 3, 1.0, 0.0).astype(BF)

    def state_part(s):
        for h in range(HEADS):
            rows = slice(HEAD * h, HEAD * h + HEAD)
            keys = phi(k_ref[s, rows, :].astype(F32)).astype(BF)
            kk[s, rows, :] = keys
            vs[s, h, :HEAD, :] = v_ref[s, rows, :]
            vs[s, h, HEAD:, :] = ones
            acc = dot(keys, vs[s, h], NTD)
            x_src[0, s, rows, :] = jnp.where(
                lane_of(acc.shape) == HEAD + 1, acc - rounded(acc), acc
            ).astype(BF)

    def rs_x(a, s):
        def make(d):
            to = along_x(d)
            return remote(
                x_src.at[a, s, pl.ds(pl.multiple_of(XR * to, 16), XR)], x_land.at[a, s, d - 1],
                ar_ss.at[a, s, d - 1], ar_rs.at[a, s, d - 1], (to * NZ + z, i),
            )

        return make

    def rs_z(a, s):
        def make(d):
            to = along_z(d)
            return remote(
                z_src.at[a, s, pl.ds(pl.multiple_of(ZR * to, 16), ZR)], z_land.at[a, s, d - 1],
                ar_ss.at[a, s, 2 + d], ar_rs.at[a, s, 2 + d], (x * NZ + to, i),
            )

        return make

    def ag_z(a, s):
        def make(d):
            mine = z_all.at[a, s, pl.ds(pl.multiple_of(ZR * z, 16), ZR)]
            return remote(
                mine, mine, ar_ss.at[a, s, 9 + d], ar_rs.at[a, s, 9 + d], (x * NZ + along_z(d), i)
            )

        return make

    def ag_x(a, s):
        whole = d_st if a else st

        def make(d):
            return remote(
                z_all.at[a, s, pl.ds(0, XR)], whole.at[s, pl.ds(pl.multiple_of(XR * x, 16), XR)],
                ar_ss.at[a, s, 16 + d], ar_rs.at[a, s, 16 + d], (along_x(d) * NZ + z, i),
            )

        return make

    def start_x(a, s):
        launch(rs_x(a, s), 1, NX, ("rx", a, s))

    def x_to_z(a, s, fix):
        arrive(("rx", a, s))
        total = x_src[a, s, pl.ds(pl.multiple_of(XR * x, 16), XR), :].astype(F32)
        for d in range(NX - 1):
            total = total + x_land[a, s, d].astype(F32)
        z_src[a, s, :XR] = fix(total).astype(BF)
        launch(rs_z(a, s), 1, NZ, ("rz", a, s))

    def z_to_all(a, s, fix):
        arrive(("rz", a, s))
        total = z_src[a, s, pl.ds(pl.multiple_of(ZR * z, 16), ZR), :].astype(F32)
        for d in range(NZ - 1):
            total = total + z_land[a, s, d].astype(F32)
        z_all[a, s, pl.ds(pl.multiple_of(ZR * z, 16), ZR), :] = fix(total).astype(BF)
        launch(ag_z(a, s), 1, NZ, ("az", a, s))

    def all_to_x(a, s):
        arrive(("az", a, s))
        launch(ag_x(a, s), 1, NX, ("ax", a, s))
        whole = d_st if a else st
        whole[s, pl.ds(pl.multiple_of(XR * x, 16), XR), :] = z_all[a, s, :XR]

    def w_plane(d):
        return remote(w_mine, w_land.at[t], w_ss.at[d - 1], w_rs.at[d - 1], (plane(d), i))

    def tree(which):
        def make(ss, rs, src, dst, step):
            return remote(src, dst, ss.at[which], rs.at[which], (t, along_y(step) * 2 + c))

        return make

    def w_rows(away, first=0, count=COLS_IP):
        return w_t.at[pl.ds(pl.multiple_of(COLS_IP * (c * NY + along_y(away)) + first, 16), count)]

    def w_near(which):
        part = w_rows(0)
        return tree(which)(wy_ss, wy_rs, part, part, (1, 7, 2, 6)[which])

    def w_far(which):
        part = w_rows((6, 2)[which])
        return tree(4 + which)(wy_ss, wy_rs, part, part, (1, 7)[which])

    def w_half(which):
        part = (w_rows(6, PART, COLS_IP - PART), w_rows(2, 0, PART))[which]
        return tree(6 + which)(wy_ss, wy_rs, part, part, (2, 6)[which])

    def w_core(d):
        mine = w_t.at[group(c * NY + along_y(d))]
        return remote(mine, mine, wc_ss.at[d], wc_rs.at[d], sib)

    def band_core(d):
        return remote(core_src.at[d], core_land.at[d], c_ss.at[d], c_rs.at[d], sib)

    def b_tree(n):
        src, dst, step = (
            lambda: (y_src.at[1], y_land.at[0], 1),
            lambda: (y_src.at[7], y_land.at[1], 7),
            lambda: (y_mid.at[0], y_land.at[2], 2),
            lambda: (y_mid.at[1], y_land.at[3], 6),
            lambda: (y_src.at[3], y_far.at[0], 1),
            lambda: (y_src.at[5], y_far.at[1], 7),
            lambda: (y_src.at[4, pl.ds(0, PART)], y_far.at[2, pl.ds(0, PART)], 2),
            lambda: (y_src.at[4, pl.ds(PART, COLS_IP - PART)], y_far.at[2, pl.ds(PART, COLS_IP - PART)], 6),
        )[n]()
        return tree(n)(y_ss, y_rs, src, dst, step)

    def gate_core():
        return remote(g_core, g_core_land, g_ss.at[0], g_rs.at[0], sib)

    def gate_y(d):
        return remote(g_src.at[group(along_y(d))], g_land.at[d - 1], g_ss.at[d], g_rs.at[d], (t, along_y(d) * 2 + c))

    def halves(column):
        high = rounded(column)
        lane = lane_of((column.shape[0], LANES)) + (FP - LANES)
        return jnp.where(lane == F, high, jnp.where(lane == F + 1, column - high, 0.0))

    def add_halves(tile):
        at = F - FP + LANES
        return halves(tile[:, at : at + 1] + tile[:, at + 1 : at + 2])

    def hot_rows(b):
        shape = (ROWS_TP, FP)
        j, lane = row_of(shape), lane_of(shape)
        at = jnp.where(j < ROWS_T, ROWS_T * b + j, jnp.where(j < ROWS_T + 2, F - ROWS_T + j, -1))
        hot_f[pl.ds(pl.multiple_of(ROWS_TP * b, 16), ROWS_TP), :] = jnp.where(lane == at, 1.0, 0.0).astype(BF)

    def hot_cols(g):
        shape = (COLS_IP, DW)
        j, lane = row_of(shape), lane_of(shape)
        first = COLS_I * (2 * (g % NY) + g // NY)
        hot_d[group(g), :] = jnp.where(lane == jnp.where(j < COLS_I, first + j, -1), 1.0, 0.0).astype(BF)

    def to_groups(b):
        rows = pl.ds(pl.multiple_of(256 * b, 16), 256)
        hot = hot_d[rows, :]
        sc_cols[rows, :] = dot(hot, scaled[...], NTD).astype(BF)
        cot_cols[rows, :] = dot(hot, cot_ref[...], NTD).astype(BF)

    def ratios(s):
        cols = slice(TOK * s, TOK * s + TOK)
        for h in range(HEADS):
            rows = slice(HEAD * h, HEAD * h + HEAD)
            both = dot(st[s, rows, :], kq[s, rows, :], TN)
            one_over = 1.0 / (both[HEAD : HEAD + 1] + both[HEAD + 1 : HEAD + 2])
            inv[s, h] = one_over
            att[rows, cols] = (both[:HEAD] * one_over).astype(BF)

    def middle(s):
        cols = slice(TOK * s, TOK * s + TOK)
        for h in range(HEADS):
            rows = slice(HEAD * h, HEAD * h + HEAD)
            d_num = rounded(d_att[rows, cols] * inv[s, h])
            d_den = -jnp.sum(d_num * att[rows, cols].astype(F32), axis=0, keepdims=True)
            high = rounded(d_den)
            row = row_of((LANES - HEAD, TOK))
            rest = jnp.where(row < 2, high, jnp.where(row == 2, d_den - high, 0.0))
            dna[s, h, :HEAD] = d_num.astype(BF)
            dna[s, h, HEAD:] = rest.astype(BF)
            acc = dot(kq[s, rows, :], dna[s, h], NTD)
            x_src[1, s, rows, :] = jnp.where(lane_of(acc.shape) == HEAD + 1, 0.0, acc).astype(BF)

    def band(first):
        rows = pl.ds(pl.multiple_of(first, 16), COLS_IP)
        return dot(sc_cols[rows, :], att[...], NTD)

    def gate_tile(first):
        rows = pl.ds(pl.multiple_of(first, 16), HALF // 2)
        part = dot(w_t[rows, :], att[...], NN) * cot_cols[rows, :].astype(F32)
        return halves(jnp.sum(part, axis=1, keepdims=True))

    def last_grads(s):
        arrive(("ax", 1, s))
        for h in range(HEADS):
            rows = slice(HEAD * h, HEAD * h + HEAD)
            keys = kk[s, rows, :]
            state = d_st[s, rows, :]
            grad = dot(state, vs[s, h], NN)
            dk_ref[s, rows, :] = (grad * jnp.minimum(keys.astype(F32), 1.0)).astype(BF)
            dv_ref[s, rows, :] = dot(state, keys, TN)[:HEAD].astype(BF)

    def pieces(b):
        total = p_sum[...]
        rows = pl.ds(pl.multiple_of(ROWS_TP * 8 * b, 16), ROWS_TP * 8)
        p_src[pl.ds(8 * b, 8)] = dot(hot_f[rows, :], total, NTD).astype(BF).reshape(8, ROWS_TP, LANES)

    def p_plane(d):
        return remote(p_src.at[plane(d)], p_land.at[d - 1], p_ss.at[d - 1], p_rs.at[d - 1], (plane(d), i))

    for a in range(2):
        for s in range(2):
            x_src[a, s, F:] = jnp.zeros((NX * XR - F, LANES), BF)
            z_src[a, s, XR:] = jnp.zeros((NZ * ZR - XR, LANES), BF)
    att[F:, :] = jnp.zeros((FP - F, 2 * TOK), BF)
    p_sum[COLS_IP:, :] = jnp.zeros((LANES - COLS_IP, FP), BF)

    pl.semaphore_wait(barrier, NT - 1 + NY - 1 + 1)
    launch(w_plane, 1, NT, "w")
    loads[0].wait()
    loads[1].wait()
    state_part(0)
    start_x(0, 0)
    state_part(1)
    start_x(0, 1)
    w_land[t] = w_mine[...]
    loop(0, NT, hot_rows)
    x_to_z(0, 0, split_sum)
    x_to_z(0, 1, split_sum)

    arrive("w")
    for b in range(FP // 384):
        cols = slice(384 * b, 384 * b + 384)
        block = dot(w_land[...].reshape(NT * ROWS_TP, LANES), hot_f[:, cols], TN)
        w_t[group(c * NY + y), cols] = block[:COLS_IP].astype(BF)
    for n in (2, 3, 0, 1):
        w_near(n).start()
    w_core(0).start()
    z_to_all(0, 0, split_sum)
    z_to_all(0, 1, split_sum)
    loop(0, 2 * NY, hot_cols)

    loads[2].wait()
    for s in range(2):
        rows = slice(TOK * s, TOK * s + TOK)
        gate = table_ref[...].reshape(1, DW) + time_ref[s]
        scaled[rows, :] = ((LOSS_SCALE * gate) * cot_ref[rows, :].astype(F32)).astype(BF)
    loop(0, DP // 256, to_groups)

    w_near(2).wait_recv()
    w_far(0).start()
    w_half(0).start()
    w_core(6).start()
    w_near(3).wait_recv()
    w_far(1).start()
    w_half(1).start()
    w_core(2).start()
    w_near(0).wait_recv()
    w_core(7).start()
    w_near(1).wait_recv()
    w_core(1).start()
    all_to_x(0, 0)
    all_to_x(0, 1)
    loads[3].wait()
    for s in range(2):
        for h in range(HEADS):
            rows = slice(HEAD * h, HEAD * h + HEAD)
            kq[s, rows, :] = phi(q_ref[s, rows, :].astype(F32)).astype(BF)

    arrive(("ax", 0, 0))
    ratios(0)
    arrive(("ax", 0, 1))
    ratios(1)

    order = (3, 5, 4, 1, 7, 2, 6, 0)
    for d in order:
        core_src[d] = band(COLS_IP * ((1 - c) * NY + along_y(d))).astype(BF)
        band_core(d).start()
    for d in order:
        own_band[d] = band(COLS_IP * (c * NY + along_y(d)))
    after = {3: (4,), 5: (5,), 4: (6, 7), 1: (0,), 7: (1,)}
    for d in order:
        band_core(d).wait_recv()
        y_src[d] = (own_band[d] + core_land[d].astype(F32)).astype(BF)
        for n in after.get(d, ()):
            b_tree(n).start()

    w_far(0).wait_recv()
    w_core(5).start()
    w_far(1).wait_recv()
    w_core(3).start()
    w_half(0).wait_recv()
    w_half(1).wait_recv()
    w_core(4).start()
    loop(0, NY, lambda d: w_core(d).wait_recv())
    for b in range(FP // 384):
        cols = slice(384 * b, 384 * b + 384)
        d_att[cols, :] = dot(w_t[:, cols], sc_cols[...], TN)
    middle(0)
    start_x(1, 0)
    middle(1)
    start_x(1, 1)

    for b in range(2):
        rows = slice(HALF // 2 * b, HALF // 2 * (b + 1))
        g_core[rows, :] = gate_tile(HALF * (1 - c) + HALF // 2 * b).astype(BF)
    gate_core().start()

    b_tree(4).wait_recv()
    b_tree(6).wait_recv()
    y_mid[0] = (y_src[2].astype(F32) + y_far[0].astype(F32)).astype(BF)
    y_mid[0, :PART] = (
        y_src[2, :PART].astype(F32) + y_far[0, :PART].astype(F32) + y_far[2, :PART].astype(F32)
    ).astype(BF)
    b_tree(2).start()
    b_tree(5).wait_recv()
    b_tree(7).wait_recv()
    y_mid[1] = (y_src[6].astype(F32) + y_far[1].astype(F32)).astype(BF)
    y_mid[1, PART:] = (
        y_src[6, PART:].astype(F32) + y_far[1, PART:].astype(F32) + y_far[2, PART:].astype(F32)
    ).astype(BF)
    b_tree(3).start()

    x_to_z(1, 0, same)
    x_to_z(1, 1, same)
    gate_core().wait_recv()
    for b in range(2):
        rows = slice(HALF // 2 * b, HALF // 2 * (b + 1))
        part = gate_tile(HALF * c + HALF // 2 * b) + g_core_land[rows, :].astype(F32)
        g_src[rows, :] = add_halves(part).astype(BF)
    launch(gate_y, 1, NY, "g")
    for s in range(2):
        for h in range(HEADS):
            rows = slice(HEAD * h, HEAD * h + HEAD)
            grad = dot(st[s, rows, :], dna[s, h], NN)
            slope = jnp.minimum(kq[s, rows, :].astype(F32), 1.0)
            dq_ref[s, rows, :] = (grad * slope).astype(BF)
    z_to_all(1, 0, same)
    z_to_all(1, 1, same)

    for n in range(4):
        b_tree(n).wait_recv()
    total = y_src[0].astype(F32)
    for d in range(4):
        total = total + y_land[d].astype(F32)
    p_sum[:COLS_IP, :] = total.astype(BF)
    arrive("g")
    gate = g_src[group(y), :].astype(F32)
    for d in range(NY - 1):
        gate = gate + g_land[d].astype(F32)
    last = total[:, FP - LANES :] + add_halves(gate)
    p_sum[:COLS_IP, FP - LANES :] = last.astype(BF)
    loop(0, NT // 8, pieces)
    launch(p_plane, 1, NT, "p")
    all_to_x(1, 0)
    all_to_x(1, 1)

    last_grads(0)
    last_grads(1)
    arrive("p")
    total = p_src[t].astype(F32)
    for d in range(NT - 1):
        total = total + p_land[d].astype(F32)
    wg_ref[...] = total[:ROWS_T, :COLS_I] * (1.0 / LOSS_SCALE)
    gate_ref[...] = total[ROWS_T : ROWS_T + 1, :COLS_I] + total[ROWS_T + 1 : ROWS_T + 2, :COLS_I]

    drain()
    for n in range(4):
        w_near(n).wait_send()
    for n in range(2):
        w_far(n).wait_send()
        w_half(n).wait_send()
    loop(0, NY, lambda d: w_core(d).wait_send())
    loop(0, NY, lambda d: band_core(d).wait_send())
    for n in range(8):
        b_tree(n).wait_send()
    gate_core().wait_send()


def on_device(query_in, key_in, value_in, cotangent, out_weight, gate_table, time_gate):
    dma = pltpu.SemaphoreType.DMA
    vm = pltpu.VMEM
    whole = pl.BlockSpec(memory_space=pltpu.VMEM)
    turned = lambda a: jnp.swapaxes(a, 2, 3).reshape(2, F, TOK)
    out = pl.pallas_call(
        kernel,
        name="linear_attention_backward",
        out_shape=[jax.ShapeDtypeStruct((2, F, TOK), BF)] * 3
        + [jax.ShapeDtypeStruct((ROWS_T, COLS_I), F32), jax.ShapeDtypeStruct((1, COLS_I), F32)],
        in_specs=[pl.BlockSpec(memory_space=pltpu.HBM)] * 4 + [whole] * 3,
        out_specs=[whole] * 5,
        scratch_shapes=[
            vm((2, F, TOK), BF),
            vm((2, F, TOK), BF),
            vm((2, HEADS, LANES, TOK), BF),
            vm((NT * ROWS_TP, FP), BF),
            vm((DP, DW), BF),
            vm((2 * TOK, DW), BF),
            vm((DP, 2 * TOK), BF),
            vm((DP, 2 * TOK), BF),
            vm((ROWS_TP, LANES), BF),
            vm((NT, ROWS_TP, LANES), BF),
            vm((DP, FP), BF),
            vm((2, NX * XR, LANES), BF),
            vm((2, NX * XR, LANES), BF),
            vm((2, 2, NX * XR, LANES), BF),
            vm((2, 2, NX - 1, XR, LANES), BF),
            vm((2, 2, NZ * ZR, LANES), BF),
            vm((2, 2, NZ - 1, ZR, LANES), BF),
            vm((2, 2, NZ * ZR, LANES), BF),
            vm((FP, 2 * TOK), F32),
            vm((FP, 2 * TOK), BF),
            vm((2, HEADS, 1, TOK), F32),
            vm((2, HEADS, LANES, TOK), BF),
            vm((NY, COLS_IP, FP), BF),
            vm((NY, COLS_IP, FP), BF),
            vm((NY, COLS_IP, FP), F32),
            vm((NY, COLS_IP, FP), BF),
            vm((4, COLS_IP, FP), BF),
            vm((2, COLS_IP, FP), BF),
            vm((3, COLS_IP, FP), BF),
            vm((LANES, FP), BF),
            vm((NT, ROWS_TP, LANES), BF),
            vm((NT - 1, ROWS_TP, LANES), BF),
            vm((HALF, LANES), BF),
            vm((HALF, LANES), BF),
            vm((HALF, LANES), BF),
            vm((NY - 1, COLS_IP, LANES), BF),
            vm((2 * TOK, DW), BF),
            vm((2, F, TOK), BF),
            vm((2, F, TOK), BF),
            vm((2, F, TOK), BF),
            dma((NT - 1,)), dma((NT - 1,)),
            dma((8,)), dma((8,)),
            dma((NY,)), dma((NY,)),
            dma((2, 2, 20)), dma((2, 2, 20)),
            dma((NY,)), dma((NY,)),
            dma((8,)), dma((8,)),
            dma((NT - 1,)), dma((NT - 1,)),
            dma((NY,)), dma((NY,)), dma((4,)),
        ],
        compiler_params=pltpu.CompilerParams(
            collective_id=0, has_side_effects=True, vmem_limit_bytes=52 * 2**20
        ),
    )(
        turned(query_in),
        turned(key_in),
        turned(value_in),
        cotangent.reshape(2 * TOK, DW),
        out_weight,
        gate_table,
        time_gate,
    )
    back = lambda a: jnp.swapaxes(a.reshape(2, 1, F, TOK), 2, 3)
    return back(out[0]), back(out[1]), back(out[2]), out[4].reshape(COLS_I), out[3]


def solution(mesh):
    big = P(None, "img", "tok", None)
    return jax.shard_map(
        on_device,
        mesh=mesh,
        in_specs=(big, big, big, big, P("tok", "img"), P(), P(None, "img", None)),
        out_specs=(big, big, big, P("img"), P("tok", "img")),
        check_vma=False,
    )
```

```python
import jax
import jax.numpy as jnp
from jax import lax
from jax.experimental import pallas as pl
from jax.experimental.pallas import tpu as pltpu
from jax.sharding import PartitionSpec as P

HEADS = 10
HEAD = 112
LOSS_SCALE = 1024.0
TOK = 128
F = 1120
DW = 1152
NX, NZ, NY = 4, 8, 8
NT = NX * NZ
LANES = 128
FP = 1152
ROWS_T = 35
ROWS_TP = 48
COLS_I = 72
COLS_IP = 80
HALF = NY * COLS_IP
DP = 2 * HALF
XR = 288
ZR = 48
PART = 48
CUT = 640
EARLY = 18
BF = jnp.bfloat16
F32 = jnp.float32
MESH = pl.DeviceIdType.MESH
NN = (((1,), (0,)), ((), ()))
NTD = (((1,), (1,)), ((), ()))
TN = (((0,), (0,)), ((), ()))


def dot(a, b, dims):
    return lax.dot_general(a, b, dims, preferred_element_type=F32)


def phi(x):
    return jnp.where(x > 0, x + 1.0, jnp.exp(jnp.minimum(x, 0.0)))


def lane_of(shape):
    return lax.broadcasted_iota(jnp.int32, shape, len(shape) - 1)


def row_of(shape):
    return lax.broadcasted_iota(jnp.int32, shape, len(shape) - 2)


def rounded(x):
    return x.astype(BF).astype(F32)


def split_sum(total):
    lane = lane_of(total.shape)
    whole = total[:, HEAD : HEAD + 1] + total[:, HEAD + 1 : HEAD + 2]
    high = rounded(whole)
    out = jnp.where((lane == HEAD) | (lane == HEAD + 2), high, total)
    return jnp.where(lane == HEAD + 1, whole - high, out)


def same(total):
    return total


def loop(first, last, body):
    def step(idx, carry):
        body(idx)
        return carry

    lax.fori_loop(first, last, step, 0)


def kernel(
    q_in, k_in, v_in, cot_in, w_in, table_in, time_in,
    dq_ref, dk_ref, dv_ref, wg_ref, gate_ref,
    kq, kk, vs, hot_f, hot_d, scaled, sc_cols, cot_cols,
    w_mine, w_land, w_t, st, d_st, x_src, x_land, z_src, z_land, z_all,
    d_att, att, inv, dna, core_src, core_land, own_band, y_src, y_land, y_mid, y_far, p_sum, g_sum, p_src, p_land,
    g_core, g_core_land, g_src, g_land, cot_ref, q_ref, k_ref, v_ref, w_ref, table_ref, time_ref,
    w_ss, w_rs, wy_ss, wy_rs, wc_ss, wc_rs, ar_ss, ar_rs, c_ss, c_rs, y_ss, y_rs, p_ss, p_rs, g_ss, g_rs, in_sem,
):
    t = lax.axis_index("tok")
    i = lax.axis_index("img")
    x, z = t // NZ, t % NZ
    y, c = i // 2, i % 2
    sib = (t, y * 2 + (1 - c))
    sends, recvs = [], {}

    def plane(d):
        return lax.rem(t + d, NT)

    def along_x(d):
        return lax.rem(x + d, NX)

    def along_z(d):
        return lax.rem(z + d, NZ)

    def along_y(d):
        return lax.rem(y + d, NY)

    def remote(src, dst, ss, rs, dev):
        return pltpu.make_async_remote_copy(
            src_ref=src, dst_ref=dst, send_sem=ss, recv_sem=rs, device_id=dev, device_id_type=MESH
        )

    def launch(make, first, last, key):
        loop(first, last, lambda d: make(d).start())
        sends.append((make, first, last))
        recvs[key] = (make, first, last)

    def arrive(key):
        make, first, last = recvs.pop(key)
        loop(first, last, lambda d: make(d).wait_recv())

    def drain():
        for key in list(recvs):
            arrive(key)
        for make, first, last in sends:
            loop(first, last, lambda d: make(d).wait_send())

    barrier = pltpu.get_barrier_semaphore()

    def greet(dev):
        pl.semaphore_signal(barrier, inc=1, device_id=dev, device_id_type=MESH)

    loads = [
        pltpu.make_async_copy(src, dst, in_sem.at[n])
        for n, (src, dst) in enumerate(
            ((k_in, k_ref), (v_in, v_ref), (cot_in, cot_ref), (q_in, q_ref), (w_in, w_ref), (table_in, table_ref), (time_in, time_ref))
        )
    ]
    for n in (4, 0, 1, 2, 3, 5, 6):
        loads[n].start()
    loop(1, NT, lambda d: greet((plane(d), i)))
    loop(1, NY, lambda d: greet((t, along_y(d) * 2 + c)))
    greet(sib)

    def group(g):
        return pl.ds(pl.multiple_of(COLS_IP * g, 16), COLS_IP)

    def head_rows(h):
        return pl.ds(pl.multiple_of(HEAD * h, 16), HEAD)

    w_mine[...] = jnp.zeros((ROWS_TP, LANES), BF)
    ones = jnp.where(row_of((LANES - HEAD, TOK)) < 3, 1.0, 0.0).astype(BF)

    def state_part(s):
        for h in range(HEADS):
            rows = slice(HEAD * h, HEAD * h + HEAD)
            keys = phi(k_ref[s, rows, :].astype(F32)).astype(BF)
            kk[s, rows, :] = keys
            vs[s, h, :HEAD, :] = v_ref[s, rows, :]
            vs[s, h, HEAD:, :] = ones
            acc = dot(keys, vs[s, h], NTD)
            x_src[0, s, rows, :] = jnp.where(
                lane_of(acc.shape) == HEAD + 1, acc - rounded(acc), acc
            ).astype(BF)

    def rs_x(a, s):
        def make(d):
            to = along_x(d)
            return remote(
                x_src.at[a, s, pl.ds(pl.multiple_of(XR * to, 16), XR)], x_land.at[a, s, d - 1],
                ar_ss.at[a, s, d - 1], ar_rs.at[a, s, d - 1], (to * NZ + z, i),
            )

        return make

    def rs_z(a, s):
        def make(d):
            to = along_z(d)
            return remote(
                z_src.at[a, s, pl.ds(pl.multiple_of(ZR * to, 16), ZR)], z_land.at[a, s, d - 1],
                ar_ss.at[a, s, 2 + d], ar_rs.at[a, s, 2 + d], (x * NZ + to, i),
            )

        return make

    def ag_z(a, s):
        def make(d):
            mine = z_all.at[a, s, pl.ds(pl.multiple_of(ZR * z, 16), ZR)]
            return remote(
                mine, mine, ar_ss.at[a, s, 9 + d], ar_rs.at[a, s, 9 + d], (x * NZ + along_z(d), i)
            )

        return make

    def ag_x(a, s):
        whole = d_st if a else st

        def make(d):
            return remote(
                z_all.at[a, s, pl.ds(0, XR)], whole.at[s, pl.ds(pl.multiple_of(XR * x, 16), XR)],
                ar_ss.at[a, s, 16 + d], ar_rs.at[a, s, 16 + d], (along_x(d) * NZ + z, i),
            )

        return make

    def start_x(a, s):
        launch(rs_x(a, s), 1, NX, ("rx", a, s))

    def x_to_z(a, s, fix):
        arrive(("rx", a, s))
        total = x_src[a, s, pl.ds(pl.multiple_of(XR * x, 16), XR), :].astype(F32)
        for d in range(NX - 1):
            total = total + x_land[a, s, d].astype(F32)
        z_src[a, s, :XR] = fix(total).astype(BF)
        launch(rs_z(a, s), 1, NZ, ("rz", a, s))

    def z_to_all(a, s, fix):
        arrive(("rz", a, s))
        total = z_src[a, s, pl.ds(pl.multiple_of(ZR * z, 16), ZR), :].astype(F32)
        for d in range(NZ - 1):
            total = total + z_land[a, s, d].astype(F32)
        z_all[a, s, pl.ds(pl.multiple_of(ZR * z, 16), ZR), :] = fix(total).astype(BF)
        launch(ag_z(a, s), 1, NZ, ("az", a, s))

    def all_to_x(a, s):
        arrive(("az", a, s))
        launch(ag_x(a, s), 1, NX, ("ax", a, s))
        whole = d_st if a else st
        whole[s, pl.ds(pl.multiple_of(XR * x, 16), XR), :] = z_all[a, s, :XR]

    def w_plane(d):
        return remote(w_mine, w_land.at[t], w_ss.at[d - 1], w_rs.at[d - 1], (plane(d), i))

    def tree(which):
        def make(ss, rs, src, dst, step):
            return remote(src, dst, ss.at[which], rs.at[which], (t, along_y(step) * 2 + c))

        return make

    def w_rows(away, first=0, count=COLS_IP):
        return w_t.at[pl.ds(pl.multiple_of(COLS_IP * (c * NY + along_y(away)) + first, 16), count)]

    def w_near(which):
        part = w_rows(0)
        return tree(which)(wy_ss, wy_rs, part, part, (1, 7, 2, 6)[which])

    def w_far(which):
        part = w_rows((6, 2)[which])
        return tree(4 + which)(wy_ss, wy_rs, part, part, (1, 7)[which])

    def w_half(which):
        part = (w_rows(6, PART, COLS_IP - PART), w_rows(2, 0, PART))[which]
        return tree(6 + which)(wy_ss, wy_rs, part, part, (2, 6)[which])

    def w_core(d):
        mine = w_t.at[group(c * NY + along_y(d))]
        return remote(mine, mine, wc_ss.at[d], wc_rs.at[d], sib)

    def band_core(d):
        return remote(core_src.at[d], core_land.at[d], c_ss.at[d], c_rs.at[d], sib)

    def b_tree(n, half):
        cols = pl.ds(CUT * half, FP - CUT if half else CUT)
        every, front, back = pl.ds(0, COLS_IP), pl.ds(0, PART), pl.ds(PART, COLS_IP - PART)
        src, dst, rows, step = (
            (y_src.at[1], y_land.at[0], every, 1),
            (y_src.at[7], y_land.at[1], every, 7),
            (y_mid.at[0], y_land.at[2], every, 2),
            (y_mid.at[1], y_land.at[3], every, 6),
            (y_src.at[3], y_far.at[0], every, 1),
            (y_src.at[5], y_far.at[1], every, 7),
            (y_src.at[4], y_far.at[2], front, 2),
            (y_src.at[4], y_far.at[2], back, 6),
        )[n]
        return tree(8 * half + n)(y_ss, y_rs, src.at[rows, cols], dst.at[rows, cols], step)

    def gate_core():
        return remote(g_core, g_core_land, g_ss.at[0], g_rs.at[0], sib)

    def gate_y(d):
        return remote(g_src.at[group(along_y(d))], g_land.at[d - 1], g_ss.at[d], g_rs.at[d], (t, along_y(d) * 2 + c))

    def halves(column):
        high = rounded(column)
        lane = lane_of((column.shape[0], LANES)) + (FP - LANES)
        return jnp.where(lane == F, high, jnp.where(lane == F + 1, column - high, 0.0))

    def add_halves(tile):
        at = F - FP + LANES
        return halves(tile[:, at : at + 1] + tile[:, at + 1 : at + 2])

    def hot_rows(b):
        shape = (ROWS_TP, FP)
        j, lane = row_of(shape), lane_of(shape)
        at = jnp.where(j < ROWS_T, ROWS_T * b + j, jnp.where(j < ROWS_T + 2, F - ROWS_T + j, -1))
        hot_f[pl.ds(pl.multiple_of(ROWS_TP * b, 16), ROWS_TP), :] = jnp.where(lane == at, 1.0, 0.0).astype(BF)

    def hot_cols(g):
        shape = (COLS_IP, DW)
        j, lane = row_of(shape), lane_of(shape)
        first = COLS_I * (2 * (g % NY) + g // NY)
        hot_d[group(g), :] = jnp.where(lane == jnp.where(j < COLS_I, first + j, -1), 1.0, 0.0).astype(BF)

    def to_groups(b):
        rows = pl.ds(pl.multiple_of(256 * b, 16), 256)
        hot = hot_d[rows, :]
        sc_cols[rows, :] = dot(hot, scaled[...], NTD).astype(BF)
        cot_cols[rows, :] = dot(hot, cot_ref[...], NTD).astype(BF)

    def ratios(s):
        cols = slice(TOK * s, TOK * s + TOK)
        for h in range(HEADS):
            rows = slice(HEAD * h, HEAD * h + HEAD)
            both = dot(st[s, rows, :], kq[s, rows, :], TN)
            one_over = 1.0 / (both[HEAD : HEAD + 1] + both[HEAD + 1 : HEAD + 2])
            inv[s, h] = one_over
            att[rows, cols] = (both[:HEAD] * one_over).astype(BF)

    def middle(s):
        cols = slice(TOK * s, TOK * s + TOK)
        for h in range(HEADS):
            rows = slice(HEAD * h, HEAD * h + HEAD)
            d_num = rounded(d_att[rows, cols] * inv[s, h])
            d_den = -jnp.sum(d_num * att[rows, cols].astype(F32), axis=0, keepdims=True)
            high = rounded(d_den)
            row = row_of((LANES - HEAD, TOK))
            rest = jnp.where(row < 2, high, jnp.where(row == 2, d_den - high, 0.0))
            dna[s, h, :HEAD] = d_num.astype(BF)
            dna[s, h, HEAD:] = rest.astype(BF)
            acc = dot(kq[s, rows, :], dna[s, h], NTD)
            x_src[1, s, rows, :] = jnp.where(lane_of(acc.shape) == HEAD + 1, 0.0, acc).astype(BF)

    def band(first):
        rows = pl.ds(pl.multiple_of(first, 16), COLS_IP)
        return dot(sc_cols[rows, :], att[...], NTD)

    def gate_tile(first):
        rows = pl.ds(pl.multiple_of(first, 16), HALF // 2)
        part = dot(w_t[rows, :], att[...], NN) * cot_cols[rows, :].astype(F32)
        return halves(jnp.sum(part, axis=1, keepdims=True))

    def last_grads(s):
        arrive(("ax", 1, s))
        for h in range(HEADS):
            rows = slice(HEAD * h, HEAD * h + HEAD)
            keys = kk[s, rows, :]
            state = d_st[s, rows, :]
            grad = dot(state, vs[s, h], NN)
            dk_ref[s, rows, :] = (grad * jnp.minimum(keys.astype(F32), 1.0)).astype(BF)
            dv_ref[s, rows, :] = dot(state, keys, TN)[:HEAD].astype(BF)

    def p_plane(d):
        return remote(p_src.at[plane(d)], p_land.at[d - 1], p_ss.at[d - 1], p_rs.at[d - 1], (plane(d), i))

    for a in range(2):
        for s in range(2):
            x_src[a, s, F:] = jnp.zeros((NX * XR - F, LANES), BF)
            z_src[a, s, XR:] = jnp.zeros((NZ * ZR - XR, LANES), BF)
    att[F:, :] = jnp.zeros((FP - F, 2 * TOK), BF)
    p_sum[COLS_IP:, :] = jnp.zeros((LANES - COLS_IP, FP), BF)
    g_sum[COLS_IP:, :] = jnp.zeros((LANES - COLS_IP, LANES), BF)

    loads[4].wait()
    w_mine[:ROWS_T, :COLS_I] = w_ref[...]
    loads[0].wait()
    loads[1].wait()
    state_part(0)
    state_part(1)
    pl.semaphore_wait(barrier, NT - 1 + NY - 1 + 1)
    start_x(0, 0)
    start_x(0, 1)
    launch(w_plane, 1, NT, "w")
    w_land[t] = w_mine[...]
    loop(0, NT, hot_rows)
    x_to_z(0, 0, split_sum)
    x_to_z(0, 1, split_sum)

    arrive("w")
    for b in range(FP // 384):
        cols = slice(384 * b, 384 * b + 384)
        block = dot(w_land[...].reshape(NT * ROWS_TP, LANES), hot_f[:, cols], TN)
        w_t[group(c * NY + y), cols] = block[:COLS_IP].astype(BF)
    for n in (2, 3, 0, 1):
        w_near(n).start()
    w_core(0).start()
    z_to_all(0, 0, split_sum)
    z_to_all(0, 1, split_sum)
    loop(0, 2 * NY, hot_cols)

    loads[2].wait()
    loads[5].wait()
    loads[6].wait()
    for s in range(2):
        rows = slice(TOK * s, TOK * s + TOK)
        gate = table_ref[...].reshape(1, DW) + time_ref[s]
        scaled[rows, :] = ((LOSS_SCALE * gate) * cot_ref[rows, :].astype(F32)).astype(BF)
    loop(0, DP // 256, to_groups)

    w_near(2).wait_recv()
    w_far(0).start()
    w_half(0).start()
    w_core(6).start()
    w_near(3).wait_recv()
    w_far(1).start()
    w_half(1).start()
    w_core(2).start()
    w_near(0).wait_recv()
    w_core(7).start()
    w_near(1).wait_recv()
    w_core(1).start()
    all_to_x(0, 0)
    all_to_x(0, 1)
    loads[3].wait()
    for s in range(2):
        for h in range(HEADS):
            rows = slice(HEAD * h, HEAD * h + HEAD)
            kq[s, rows, :] = phi(q_ref[s, rows, :].astype(F32)).astype(BF)

    arrive(("ax", 0, 0))
    ratios(0)
    arrive(("ax", 0, 1))
    ratios(1)

    order = (3, 5, 4, 1, 7, 2, 6, 0)
    for d in order:
        core_src[d] = band(COLS_IP * ((1 - c) * NY + along_y(d))).astype(BF)
        band_core(d).start()
    for d in order:
        own_band[d] = band(COLS_IP * (c * NY + along_y(d)))
    after = {
        3: ((4, 0),),
        5: ((5, 0),),
        4: ((6, 0), (7, 0), (4, 1), (5, 1), (6, 1), (7, 1)),
        1: ((0, 0),),
        7: ((1, 0), (0, 1), (1, 1)),
    }
    for d in order:
        band_core(d).wait_recv()
        y_src[d] = (own_band[d] + core_land[d].astype(F32)).astype(BF)
        for n, half in after.get(d, ()):
            b_tree(n, half).start()

    w_far(0).wait_recv()
    w_core(5).start()
    w_far(1).wait_recv()
    w_core(3).start()
    w_half(0).wait_recv()
    w_half(1).wait_recv()
    w_core(4).start()
    loop(0, NY, lambda d: w_core(d).wait_recv())
    for b in range(FP // 384):
        cols = slice(384 * b, 384 * b + 384)
        d_att[cols, :] = dot(w_t[:, cols], sc_cols[...], TN)
    middle(0)
    start_x(1, 0)
    middle(1)
    start_x(1, 1)

    for half in range(2):
        cols = slice(CUT * half, FP if half else CUT)
        for n, near, rows in ((0, 2, slice(0, PART)), (1, 6, slice(PART, COLS_IP))):
            b_tree(4 + n, half).wait_recv()
            b_tree(6 + n, half).wait_recv()
            part = y_src[near, :, cols].astype(F32) + y_far[n, :, cols].astype(F32)
            y_mid[n, :, cols] = part.astype(BF)
            y_mid[n, rows, cols] = (part[rows] + y_far[2, rows, cols].astype(F32)).astype(BF)
            b_tree(2 + n, half).start()

    for b in range(2):
        rows = slice(HALF // 2 * b, HALF // 2 * (b + 1))
        g_core[rows, :] = gate_tile(HALF * (1 - c) + HALF // 2 * b).astype(BF)
    gate_core().start()

    x_to_z(1, 0, same)
    x_to_z(1, 1, same)
    gate_core().wait_recv()
    for b in range(2):
        rows = slice(HALF // 2 * b, HALF // 2 * (b + 1))
        part = gate_tile(HALF * c + HALF // 2 * b) + g_core_land[rows, :].astype(F32)
        g_src[rows, :] = add_halves(part).astype(BF)
    launch(gate_y, 1, NY, "g")
    for s in range(2):
        for h in range(HEADS):
            rows = slice(HEAD * h, HEAD * h + HEAD)
            grad = dot(st[s, rows, :], dna[s, h], NN)
            slope = jnp.minimum(kq[s, rows, :].astype(F32), 1.0)
            dq_ref[s, rows, :] = (grad * slope).astype(BF)
    z_to_all(1, 0, same)
    z_to_all(1, 1, same)

    def y_total(half):
        cols = slice(CUT * half, FP if half else CUT)
        for n in range(4):
            b_tree(n, half).wait_recv()
        total = y_src[0, :, cols].astype(F32)
        for d in range(4):
            total = total + y_land[d, :, cols].astype(F32)
        p_sum[:COLS_IP, cols] = total.astype(BF)

    def send_piece(to):
        @pl.when(to != t)
        def _():
            p_plane(lax.rem(to - t + NT, NT)).start()

    y_total(0)
    arrive("g")
    gate = g_src[group(y), :].astype(F32)
    for d in range(NY - 1):
        gate = gate + g_land[d].astype(F32)
    g_sum[:COLS_IP, :] = add_halves(gate).astype(BF)

    def early(b):
        rows = pl.ds(pl.multiple_of(ROWS_TP * 6 * b, 16), ROWS_TP * 6)
        block = dot(hot_f[rows, :CUT], p_sum[:, :CUT], NTD) + dot(hot_f[rows, FP - LANES :], g_sum[...], NTD)
        p_src[pl.ds(6 * b, 6)] = block.astype(BF).reshape(6, ROWS_TP, LANES)

    loop(0, EARLY // 6, early)
    loop(0, EARLY, send_piece)
    y_total(1)
    p_sum[:COLS_IP, FP - LANES :] = p_sum[:COLS_IP, FP - LANES :] + g_sum[:COLS_IP, :]

    def late(b):
        rows = pl.ds(pl.multiple_of(ROWS_TP * (EARLY + 7 * b), 16), ROWS_TP * 7)
        block = dot(hot_f[rows, CUT - LANES :], p_sum[:, CUT - LANES :], NTD)
        p_src[pl.ds(EARLY + 7 * b, 7)] = block.astype(BF).reshape(7, ROWS_TP, LANES)

    loop(0, (NT - EARLY) // 7, late)
    loop(EARLY, NT, send_piece)
    sends.append((p_plane, 1, NT))
    recvs["p"] = (p_plane, 1, NT)
    all_to_x(1, 0)
    all_to_x(1, 1)

    last_grads(0)
    last_grads(1)
    arrive("p")
    total = p_src[t].astype(F32)
    for d in range(NT - 1):
        total = total + p_land[d].astype(F32)
    wg_ref[...] = total[:ROWS_T, :COLS_I] * (1.0 / LOSS_SCALE)
    gate_ref[...] = total[ROWS_T : ROWS_T + 1, :COLS_I] + total[ROWS_T + 1 : ROWS_T + 2, :COLS_I]

    drain()
    for n in range(4):
        w_near(n).wait_send()
    for n in range(2):
        w_far(n).wait_send()
        w_half(n).wait_send()
    loop(0, NY, lambda d: w_core(d).wait_send())
    loop(0, NY, lambda d: band_core(d).wait_send())
    for n in range(8):
        for half in range(2):
            b_tree(n, half).wait_send()
    gate_core().wait_send()


def on_device(query_in, key_in, value_in, cotangent, out_weight, gate_table, time_gate):
    dma = pltpu.SemaphoreType.DMA
    vm = pltpu.VMEM
    whole = pl.BlockSpec(memory_space=pltpu.VMEM)
    turned = lambda a: jnp.swapaxes(a, 2, 3).reshape(2, F, TOK)
    out = pl.pallas_call(
        kernel,
        name="linear_attention_backward",
        out_shape=[jax.ShapeDtypeStruct((2, F, TOK), BF)] * 3
        + [jax.ShapeDtypeStruct((ROWS_T, COLS_I), F32), jax.ShapeDtypeStruct((1, COLS_I), F32)],
        in_specs=[pl.BlockSpec(memory_space=pltpu.HBM)] * 7,
        out_specs=[whole] * 5,
        scratch_shapes=[
            vm((2, F, TOK), BF),
            vm((2, F, TOK), BF),
            vm((2, HEADS, LANES, TOK), BF),
            vm((NT * ROWS_TP, FP), BF),
            vm((DP, DW), BF),
            vm((2 * TOK, DW), BF),
            vm((DP, 2 * TOK), BF),
            vm((DP, 2 * TOK), BF),
            vm((ROWS_TP, LANES), BF),
            vm((NT, ROWS_TP, LANES), BF),
            vm((DP, FP), BF),
            vm((2, NX * XR, LANES), BF),
            vm((2, NX * XR, LANES), BF),
            vm((2, 2, NX * XR, LANES), BF),
            vm((2, 2, NX - 1, XR, LANES), BF),
            vm((2, 2, NZ * ZR, LANES), BF),
            vm((2, 2, NZ - 1, ZR, LANES), BF),
            vm((2, 2, NZ * ZR, LANES), BF),
            vm((FP, 2 * TOK), F32),
            vm((FP, 2 * TOK), BF),
            vm((2, HEADS, 1, TOK), F32),
            vm((2, HEADS, LANES, TOK), BF),
            vm((NY, COLS_IP, FP), BF),
            vm((NY, COLS_IP, FP), BF),
            vm((NY, COLS_IP, FP), F32),
            vm((NY, COLS_IP, FP), BF),
            vm((4, COLS_IP, FP), BF),
            vm((2, COLS_IP, FP), BF),
            vm((3, COLS_IP, FP), BF),
            vm((LANES, FP), BF),
            vm((LANES, LANES), BF),
            vm((NT, ROWS_TP, LANES), BF),
            vm((NT - 1, ROWS_TP, LANES), BF),
            vm((HALF, LANES), BF),
            vm((HALF, LANES), BF),
            vm((HALF, LANES), BF),
            vm((NY - 1, COLS_IP, LANES), BF),
            vm((2 * TOK, DW), BF),
            vm((2, F, TOK), BF),
            vm((2, F, TOK), BF),
            vm((2, F, TOK), BF),
            vm((ROWS_T, COLS_I), BF),
            vm((DW,), F32),
            vm((2, 1, DW), F32),
            dma((NT - 1,)), dma((NT - 1,)),
            dma((8,)), dma((8,)),
            dma((NY,)), dma((NY,)),
            dma((2, 2, 20)), dma((2, 2, 20)),
            dma((NY,)), dma((NY,)),
            dma((16,)), dma((16,)),
            dma((NT - 1,)), dma((NT - 1,)),
            dma((NY,)), dma((NY,)), dma((7,)),
        ],
        compiler_params=pltpu.CompilerParams(
            collective_id=0, has_side_effects=True, vmem_limit_bytes=52 * 2**20
        ),
    )(
        turned(query_in),
        turned(key_in),
        turned(value_in),
        cotangent.reshape(2 * TOK, DW),
        out_weight,
        gate_table,
        time_gate,
    )
    back = lambda a: jnp.swapaxes(a.reshape(2, 1, F, TOK), 2, 3)
    return back(out[0]), back(out[1]), back(out[2]), out[4].reshape(COLS_I), out[3]


def solution(mesh):
    big = P(None, "img", "tok", None)
    return jax.shard_map(
        on_device,
        mesh=mesh,
        in_specs=(big, big, big, big, P("tok", "img"), P(), P(None, "img", None)),
        out_specs=(big, big, big, P("img"), P("tok", "img")),
        check_vma=False,
    )
```

```python
import jax
import jax.numpy as jnp
from jax import lax
from jax.experimental import pallas as pl
from jax.experimental.pallas import tpu as pltpu
from jax.sharding import PartitionSpec as P

HEADS = 10
HEAD = 112
LOSS_SCALE = 1024.0
TOK = 128
F = 1120
DW = 1152
NX, NZ, NY = 4, 8, 8
NT = NX * NZ
LANES = 128
FP = 1152
ROWS_T = 35
ROWS_TP = 48
COLS_I = 72
COLS_IP = 80
HALF = NY * COLS_IP
DP = 2 * HALF
XR = 288
ZR = 48
PART = 48
CUT = 640
EARLY = 18
BF = jnp.bfloat16
F32 = jnp.float32
MESH = pl.DeviceIdType.MESH
NN = (((1,), (0,)), ((), ()))
NTD = (((1,), (1,)), ((), ()))
TN = (((0,), (0,)), ((), ()))


def dot(a, b, dims):
    return lax.dot_general(a, b, dims, preferred_element_type=F32)


def phi(x):
    return jnp.where(x > 0, x + 1.0, jnp.exp(jnp.minimum(x, 0.0)))


def lane_of(shape):
    return lax.broadcasted_iota(jnp.int32, shape, len(shape) - 1)


def row_of(shape):
    return lax.broadcasted_iota(jnp.int32, shape, len(shape) - 2)


def rounded(x):
    return x.astype(BF).astype(F32)


def split_sum(total):
    lane = lane_of(total.shape)
    whole = total[:, HEAD : HEAD + 1] + total[:, HEAD + 1 : HEAD + 2]
    high = rounded(whole)
    out = jnp.where((lane == HEAD) | (lane == HEAD + 2), high, total)
    return jnp.where(lane == HEAD + 1, whole - high, out)


def same(total):
    return total


def loop(first, last, body):
    def step(idx, carry):
        body(idx)
        return carry

    lax.fori_loop(first, last, step, 0)


def kernel(
    q_in, k_in, v_in, cot_in, w_in, table_in, time_in,
    dq_ref, dk_ref, dv_ref, wg_ref, gate_ref,
    kq, kk, vs, hot_f, hot_d, scaled, sc_cols, cot_cols,
    w_mine, w_land, w_t, st, d_st, x_src, x_land, z_src, z_land, z_all,
    d_att, att, inv, dna, core_src, core_land, own_band, y_src, y_land, y_mid, y_far, p_sum, g_sum, p_src, p_land,
    g_core, g_core_land, g_src, g_land, cot_ref, q_ref, k_ref, v_ref, w_ref, table_ref, time_ref,
    w_ss, w_rs, wy_ss, wy_rs, wc_ss, wc_rs, ar_ss, ar_rs, c_ss, c_rs, y_ss, y_rs, p_ss, p_rs, g_ss, g_rs, in_sem,
):
    t = lax.axis_index("tok")
    i = lax.axis_index("img")
    x, z = t // NZ, t % NZ
    y, c = i // 2, i % 2
    sib = (t, y * 2 + (1 - c))
    sends, recvs = [], {}

    def plane(d):
        return lax.rem(t + d, NT)

    def along_x(d):
        return lax.rem(x + d, NX)

    def along_z(d):
        return lax.rem(z + d, NZ)

    def along_y(d):
        return lax.rem(y + d, NY)

    def remote(src, dst, ss, rs, dev):
        return pltpu.make_async_remote_copy(
            src_ref=src, dst_ref=dst, send_sem=ss, recv_sem=rs, device_id=dev, device_id_type=MESH
        )

    def launch(make, first, last, key):
        loop(first, last, lambda d: make(d).start())
        sends.append((make, first, last))
        recvs[key] = (make, first, last)

    def arrive(key):
        make, first, last = recvs.pop(key)
        loop(first, last, lambda d: make(d).wait_recv())

    def drain_sends():
        for make, first, last in sends:
            loop(first, last, lambda d: make(d).wait_send())

    barrier = pltpu.get_barrier_semaphore()

    def greet(dev):
        pl.semaphore_signal(barrier, inc=1, device_id=dev, device_id_type=MESH)

    loads = [
        pltpu.make_async_copy(src, dst, in_sem.at[n])
        for n, (src, dst) in enumerate(
            ((k_in, k_ref), (v_in, v_ref), (cot_in, cot_ref), (q_in, q_ref), (w_in, w_ref), (table_in, table_ref), (time_in, time_ref))
        )
    ]
    for n in (4, 0, 1, 2, 3, 5, 6):
        loads[n].start()
    for d in range(1, NT):
        greet((plane(d), i))
    for d in range(1, NY):
        greet((t, along_y(d) * 2 + c))
    greet(sib)

    def group(g):
        return pl.ds(pl.multiple_of(COLS_IP * g, 16), COLS_IP)

    def head_rows(h):
        return pl.ds(pl.multiple_of(HEAD * h, 16), HEAD)

    w_mine[...] = jnp.zeros((ROWS_TP, LANES), BF)
    ones = jnp.where(row_of((LANES - HEAD, TOK)) < 3, 1.0, 0.0).astype(BF)

    def state_part(s):
        for h in range(HEADS):
            rows = slice(HEAD * h, HEAD * h + HEAD)
            keys = phi(k_ref[s, rows, :].astype(F32)).astype(BF)
            kk[s, rows, :] = keys
            vs[s, h, :HEAD, :] = v_ref[s, rows, :]
            vs[s, h, HEAD:, :] = ones
            acc = dot(keys, vs[s, h], NTD)
            x_src[0, s, rows, :] = jnp.where(
                lane_of(acc.shape) == HEAD + 1, acc - rounded(acc), acc
            ).astype(BF)

    def rs_x(a, s):
        def make(d):
            to = along_x(d)
            return remote(
                x_src.at[a, s, pl.ds(pl.multiple_of(XR * to, 16), XR)], x_land.at[a, s, d - 1],
                ar_ss.at[a, s, d - 1], ar_rs.at[a, s, d - 1], (to * NZ + z, i),
            )

        return make

    def rs_z(a, s):
        def make(d):
            to = along_z(d)
            return remote(
                z_src.at[a, s, pl.ds(pl.multiple_of(ZR * to, 16), ZR)], z_land.at[a, s, d - 1],
                ar_ss.at[a, s, 2 + d], ar_rs.at[a, s, 2 + d], (x * NZ + to, i),
            )

        return make

    def ag_z(a, s):
        def make(d):
            mine = z_all.at[a, s, pl.ds(pl.multiple_of(ZR * z, 16), ZR)]
            return remote(
                mine, mine, ar_ss.at[a, s, 9 + d], ar_rs.at[a, s, 9 + d], (x * NZ + along_z(d), i)
            )

        return make

    def ag_x(a, s):
        whole = d_st if a else st

        def make(d):
            return remote(
                z_all.at[a, s, pl.ds(0, XR)], whole.at[s, pl.ds(pl.multiple_of(XR * x, 16), XR)],
                ar_ss.at[a, s, 16 + d], ar_rs.at[a, s, 16 + d], (along_x(d) * NZ + z, i),
            )

        return make

    def start_x(a, s):
        launch(rs_x(a, s), 1, NX, ("rx", a, s))

    def x_to_z(a, s, fix):
        arrive(("rx", a, s))
        total = x_src[a, s, pl.ds(pl.multiple_of(XR * x, 16), XR), :].astype(F32)
        for d in range(NX - 1):
            total = total + x_land[a, s, d].astype(F32)
        z_src[a, s, :XR] = fix(total).astype(BF)
        launch(rs_z(a, s), 1, NZ, ("rz", a, s))

    def z_to_all(a, s, fix):
        arrive(("rz", a, s))
        total = z_src[a, s, pl.ds(pl.multiple_of(ZR * z, 16), ZR), :].astype(F32)
        for d in range(NZ - 1):
            total = total + z_land[a, s, d].astype(F32)
        z_all[a, s, pl.ds(pl.multiple_of(ZR * z, 16), ZR), :] = fix(total).astype(BF)
        launch(ag_z(a, s), 1, NZ, ("az", a, s))

    def all_to_x(a, s):
        arrive(("az", a, s))
        launch(ag_x(a, s), 1, NX, ("ax", a, s))
        whole = d_st if a else st
        whole[s, pl.ds(pl.multiple_of(XR * x, 16), XR), :] = z_all[a, s, :XR]

    def w_plane(d):
        return remote(w_mine, w_land.at[t], w_ss.at[d - 1], w_rs.at[d - 1], (plane(d), i))

    def tree(which):
        def make(ss, rs, src, dst, step):
            return remote(src, dst, ss.at[which], rs.at[which], (t, along_y(step) * 2 + c))

        return make

    def w_rows(away, first=0, count=COLS_IP):
        return w_t.at[pl.ds(pl.multiple_of(COLS_IP * (c * NY + along_y(away)) + first, 16), count)]

    def w_near(which):
        part = w_rows(0)
        return tree(which)(wy_ss, wy_rs, part, part, (1, 7, 2, 6)[which])

    def w_far(which):
        part = w_rows((6, 2)[which])
        return tree(4 + which)(wy_ss, wy_rs, part, part, (1, 7)[which])

    def w_half(which):
        part = (w_rows(6, PART, COLS_IP - PART), w_rows(2, 0, PART))[which]
        return tree(6 + which)(wy_ss, wy_rs, part, part, (2, 6)[which])

    def w_core(d):
        mine = w_t.at[group(c * NY + along_y(d))]
        return remote(mine, mine, wc_ss.at[d], wc_rs.at[d], sib)

    def band_core(d):
        return remote(core_src.at[d], core_land.at[d], c_ss.at[d], c_rs.at[d], sib)

    def b_tree(n, half):
        cols = pl.ds(CUT * half, FP - CUT if half else CUT)
        every, front, back = pl.ds(0, COLS_IP), pl.ds(0, PART), pl.ds(PART, COLS_IP - PART)
        src, dst, rows, step = (
            (y_src.at[1], y_land.at[0], every, 1),
            (y_src.at[7], y_land.at[1], every, 7),
            (y_mid.at[0], y_land.at[2], every, 2),
            (y_mid.at[1], y_land.at[3], every, 6),
            (y_src.at[3], y_far.at[0], every, 1),
            (y_src.at[5], y_far.at[1], every, 7),
            (y_src.at[4], y_far.at[2], front, 2),
            (y_src.at[4], y_far.at[2], back, 6),
        )[n]
        return tree(8 * half + n)(y_ss, y_rs, src.at[rows, cols], dst.at[rows, cols], step)

    def gate_core():
        return remote(g_core, g_core_land, g_ss.at[0], g_rs.at[0], sib)

    def gate_y(d):
        return remote(g_src.at[group(along_y(d))], g_land.at[d - 1], g_ss.at[d], g_rs.at[d], (t, along_y(d) * 2 + c))

    def halves(column):
        high = rounded(column)
        lane = lane_of((column.shape[0], LANES)) + (FP - LANES)
        return jnp.where(lane == F, high, jnp.where(lane == F + 1, column - high, 0.0))

    def add_halves(tile):
        at = F - FP + LANES
        return halves(tile[:, at : at + 1] + tile[:, at + 1 : at + 2])

    def hot_rows(b):
        shape = (ROWS_TP, FP)
        j, lane = row_of(shape), lane_of(shape)
        at = jnp.where(j < ROWS_T, ROWS_T * b + j, jnp.where(j < ROWS_T + 2, F - ROWS_T + j, -1))
        hot_f[pl.ds(pl.multiple_of(ROWS_TP * b, 16), ROWS_TP), :] = jnp.where(lane == at, 1.0, 0.0).astype(BF)

    def hot_cols(g):
        shape = (COLS_IP, DW)
        j, lane = row_of(shape), lane_of(shape)
        first = COLS_I * (2 * (g % NY) + g // NY)
        hot_d[group(g), :] = jnp.where(lane == jnp.where(j < COLS_I, first + j, -1), 1.0, 0.0).astype(BF)

    def to_groups(b):
        rows = pl.ds(pl.multiple_of(256 * b, 16), 256)
        hot = hot_d[rows, :]
        sc_cols[rows, :] = dot(hot, scaled[...], NTD).astype(BF)
        cot_cols[rows, :] = dot(hot, cot_ref[...], NTD).astype(BF)

    def ratios(s):
        cols = slice(TOK * s, TOK * s + TOK)
        for h in range(HEADS):
            rows = slice(HEAD * h, HEAD * h + HEAD)
            both = dot(st[s, rows, :], kq[s, rows, :], TN)
            one_over = 1.0 / (both[HEAD : HEAD + 1] + both[HEAD + 1 : HEAD + 2])
            inv[s, h] = one_over
            att[rows, cols] = (both[:HEAD] * one_over).astype(BF)

    def middle(s):
        cols = slice(TOK * s, TOK * s + TOK)
        for h in range(HEADS):
            rows = slice(HEAD * h, HEAD * h + HEAD)
            d_num = rounded(d_att[rows, cols] * inv[s, h])
            d_den = -jnp.sum(d_num * att[rows, cols].astype(F32), axis=0, keepdims=True)
            high = rounded(d_den)
            row = row_of((LANES - HEAD, TOK))
            rest = jnp.where(row < 2, high, jnp.where(row == 2, d_den - high, 0.0))
            dna[s, h, :HEAD] = d_num.astype(BF)
            dna[s, h, HEAD:] = rest.astype(BF)
            acc = dot(kq[s, rows, :], dna[s, h], NTD)
            x_src[1, s, rows, :] = jnp.where(lane_of(acc.shape) == HEAD + 1, 0.0, acc).astype(BF)

    def band(first):
        rows = pl.ds(pl.multiple_of(first, 16), COLS_IP)
        return dot(sc_cols[rows, :], att[...], NTD)

    def gate_tile(first):
        rows = pl.ds(pl.multiple_of(first, 16), HALF // 2)
        part = dot(w_t[rows, :], att[...], NN) * cot_cols[rows, :].astype(F32)
        return halves(jnp.sum(part, axis=1, keepdims=True))

    def last_grads(s):
        arrive(("ax", 1, s))
        for h in range(HEADS):
            rows = slice(HEAD * h, HEAD * h + HEAD)
            keys = kk[s, rows, :]
            state = d_st[s, rows, :]
            grad = dot(state, vs[s, h], NN)
            dk_ref[s, rows, :] = (grad * jnp.minimum(keys.astype(F32), 1.0)).astype(BF)
            dv_ref[s, rows, :] = dot(state, keys, TN)[:HEAD].astype(BF)

    def p_plane(d):
        return remote(p_src.at[plane(d)], p_land.at[d - 1], p_ss.at[d - 1], p_rs.at[d - 1], (plane(d), i))

    for a in range(2):
        for s in range(2):
            x_src[a, s, F:] = jnp.zeros((NX * XR - F, LANES), BF)
            z_src[a, s, XR:] = jnp.zeros((NZ * ZR - XR, LANES), BF)
    att[F:, :] = jnp.zeros((FP - F, 2 * TOK), BF)
    p_sum[COLS_IP:, :] = jnp.zeros((LANES - COLS_IP, FP), BF)
    g_sum[COLS_IP:, :] = jnp.zeros((LANES - COLS_IP, LANES), BF)

    loads[4].wait()
    w_mine[:ROWS_T, :COLS_I] = w_ref[...]
    loads[0].wait()
    loads[1].wait()
    state_part(0)
    state_part(1)
    pl.semaphore_wait(barrier, NT - 1 + NY - 1 + 1)
    start_x(0, 0)
    start_x(0, 1)
    launch(w_plane, 1, NT, "w")
    w_land[t] = w_mine[...]
    loop(0, NT, hot_rows)
    x_to_z(0, 0, split_sum)
    x_to_z(0, 1, split_sum)

    arrive("w")
    for b in range(FP // 384):
        cols = slice(384 * b, 384 * b + 384)
        block = dot(w_land[...].reshape(NT * ROWS_TP, LANES), hot_f[:, cols], TN)
        w_t[group(c * NY + y), cols] = block[:COLS_IP].astype(BF)
    for n in (2, 3, 0, 1):
        w_near(n).start()
    w_core(0).start()
    z_to_all(0, 0, split_sum)
    z_to_all(0, 1, split_sum)
    loop(0, 2 * NY, hot_cols)

    loads[2].wait()
    loads[5].wait()
    loads[6].wait()
    for s in range(2):
        rows = slice(TOK * s, TOK * s + TOK)
        gate = table_ref[...].reshape(1, DW) + time_ref[s]
        scaled[rows, :] = ((LOSS_SCALE * gate) * cot_ref[rows, :].astype(F32)).astype(BF)
    loop(0, DP // 256, to_groups)

    w_near(2).wait_recv()
    w_far(0).start()
    w_half(0).start()
    w_core(6).start()
    w_near(3).wait_recv()
    w_far(1).start()
    w_half(1).start()
    w_core(2).start()
    w_near(0).wait_recv()
    w_core(7).start()
    w_near(1).wait_recv()
    w_core(1).start()
    all_to_x(0, 0)
    all_to_x(0, 1)
    loads[3].wait()
    for s in range(2):
        for h in range(HEADS):
            rows = slice(HEAD * h, HEAD * h + HEAD)
            kq[s, rows, :] = phi(q_ref[s, rows, :].astype(F32)).astype(BF)

    arrive(("ax", 0, 0))
    ratios(0)
    arrive(("ax", 0, 1))
    ratios(1)

    order = (3, 5, 4, 1, 7, 2, 6, 0)
    for d in order:
        core_src[d] = band(COLS_IP * ((1 - c) * NY + along_y(d))).astype(BF)
        band_core(d).start()
    for d in order:
        own_band[d] = band(COLS_IP * (c * NY + along_y(d)))
    after = {
        3: ((4, 0),),
        5: ((5, 0),),
        4: ((6, 0), (7, 0), (4, 1), (5, 1), (6, 1), (7, 1)),
        1: ((0, 0),),
        7: ((1, 0), (0, 1), (1, 1)),
    }
    for d in order:
        band_core(d).wait_recv()
        y_src[d] = (own_band[d] + core_land[d].astype(F32)).astype(BF)
        for n, half in after.get(d, ()):
            b_tree(n, half).start()

    w_far(0).wait_recv()
    w_core(5).start()
    w_far(1).wait_recv()
    w_core(3).start()
    w_half(0).wait_recv()
    w_half(1).wait_recv()
    w_core(4).start()
    loop(0, NY, lambda d: w_core(d).wait_recv())
    for b in range(FP // 384):
        cols = slice(384 * b, 384 * b + 384)
        d_att[cols, :] = dot(w_t[:, cols], sc_cols[...], TN)
    middle(0)
    start_x(1, 0)
    middle(1)
    start_x(1, 1)

    for half in range(2):
        cols = slice(CUT * half, FP if half else CUT)
        for n, near, rows in ((0, 2, slice(0, PART)), (1, 6, slice(PART, COLS_IP))):
            b_tree(4 + n, half).wait_recv()
            b_tree(6 + n, half).wait_recv()
            part = y_src[near, :, cols].astype(F32) + y_far[n, :, cols].astype(F32)
            y_mid[n, :, cols] = part.astype(BF)
            y_mid[n, rows, cols] = (part[rows] + y_far[2, rows, cols].astype(F32)).astype(BF)
            b_tree(2 + n, half).start()

    for b in range(2):
        rows = slice(HALF // 2 * b, HALF // 2 * (b + 1))
        g_core[rows, :] = gate_tile(HALF * (1 - c) + HALF // 2 * b).astype(BF)
    gate_core().start()

    x_to_z(1, 0, same)
    x_to_z(1, 1, same)
    gate_core().wait_recv()
    for b in range(2):
        rows = slice(HALF // 2 * b, HALF // 2 * (b + 1))
        part = gate_tile(HALF * c + HALF // 2 * b) + g_core_land[rows, :].astype(F32)
        g_src[rows, :] = add_halves(part).astype(BF)
    launch(gate_y, 1, NY, "g")
    for s in range(2):
        for h in range(HEADS):
            rows = slice(HEAD * h, HEAD * h + HEAD)
            grad = dot(st[s, rows, :], dna[s, h], NN)
            slope = jnp.minimum(kq[s, rows, :].astype(F32), 1.0)
            dq_ref[s, rows, :] = (grad * slope).astype(BF)
    z_to_all(1, 0, same)
    z_to_all(1, 1, same)

    def y_total(half):
        cols = slice(CUT * half, FP if half else CUT)
        for n in range(4):
            b_tree(n, half).wait_recv()
        total = y_src[0, :, cols].astype(F32)
        for d in range(4):
            total = total + y_land[d, :, cols].astype(F32)
        p_sum[:COLS_IP, cols] = total.astype(BF)

    def send_piece(to):
        @pl.when(to != t)
        def _():
            p_plane(lax.rem(to - t + NT, NT)).start()

    y_total(0)
    arrive("g")
    gate = g_src[group(y), :].astype(F32)
    for d in range(NY - 1):
        gate = gate + g_land[d].astype(F32)
    g_sum[:COLS_IP, :] = add_halves(gate).astype(BF)

    def early(b):
        rows = pl.ds(pl.multiple_of(ROWS_TP * 6 * b, 16), ROWS_TP * 6)
        block = dot(hot_f[rows, :CUT], p_sum[:, :CUT], NTD) + dot(hot_f[rows, FP - LANES :], g_sum[...], NTD)
        p_src[pl.ds(6 * b, 6)] = block.astype(BF).reshape(6, ROWS_TP, LANES)

    loop(0, EARLY // 6, early)
    loop(0, EARLY, send_piece)
    y_total(1)
    p_sum[:COLS_IP, FP - LANES :] = p_sum[:COLS_IP, FP - LANES :] + g_sum[:COLS_IP, :]

    def late(b):
        rows = pl.ds(pl.multiple_of(ROWS_TP * (EARLY + 7 * b), 16), ROWS_TP * 7)
        block = dot(hot_f[rows, CUT - LANES :], p_sum[:, CUT - LANES :], NTD)
        p_src[pl.ds(EARLY + 7 * b, 7)] = block.astype(BF).reshape(7, ROWS_TP, LANES)

    loop(0, (NT - EARLY) // 7, late)
    loop(EARLY, NT, send_piece)
    sends.append((p_plane, 1, NT))
    all_to_x(1, 0)
    all_to_x(1, 1)

    last_grads(0)
    last_grads(1)
    drain_sends()
    for n in range(4):
        w_near(n).wait_send()
    for n in range(2):
        w_far(n).wait_send()
        w_half(n).wait_send()
    loop(0, NY, lambda d: w_core(d).wait_send())
    loop(0, NY, lambda d: band_core(d).wait_send())
    for n in range(8):
        for half in range(2):
            b_tree(n, half).wait_send()
    gate_core().wait_send()

    for d in range(1, NT):
        p_plane(d).wait_recv()
    total = p_src[t].astype(F32)
    for d in range(NT - 1):
        total = total + p_land[d].astype(F32)
    wg_ref[...] = total[:ROWS_T, :COLS_I] * (1.0 / LOSS_SCALE)
    gate_ref[...] = total[ROWS_T : ROWS_T + 1, :COLS_I] + total[ROWS_T + 1 : ROWS_T + 2, :COLS_I]


def on_device(query_in, key_in, value_in, cotangent, out_weight, gate_table, time_gate):
    dma = pltpu.SemaphoreType.DMA
    vm = pltpu.VMEM
    whole = pl.BlockSpec(memory_space=pltpu.VMEM)
    turned = lambda a: jnp.swapaxes(a, 2, 3).reshape(2, F, TOK)
    out = pl.pallas_call(
        kernel,
        name="linear_attention_backward",
        out_shape=[jax.ShapeDtypeStruct((2, F, TOK), BF)] * 3
        + [jax.ShapeDtypeStruct((ROWS_T, COLS_I), F32), jax.ShapeDtypeStruct((1, COLS_I), F32)],
        in_specs=[pl.BlockSpec(memory_space=pltpu.HBM)] * 7,
        out_specs=[whole] * 5,
        scratch_shapes=[
            vm((2, F, TOK), BF),
            vm((2, F, TOK), BF),
            vm((2, HEADS, LANES, TOK), BF),
            vm((NT * ROWS_TP, FP), BF),
            vm((DP, DW), BF),
            vm((2 * TOK, DW), BF),
            vm((DP, 2 * TOK), BF),
            vm((DP, 2 * TOK), BF),
            vm((ROWS_TP, LANES), BF),
            vm((NT, ROWS_TP, LANES), BF),
            vm((DP, FP), BF),
            vm((2, NX * XR, LANES), BF),
            vm((2, NX * XR, LANES), BF),
            vm((2, 2, NX * XR, LANES), BF),
            vm((2, 2, NX - 1, XR, LANES), BF),
            vm((2, 2, NZ * ZR, LANES), BF),
            vm((2, 2, NZ - 1, ZR, LANES), BF),
            vm((2, 2, NZ * ZR, LANES), BF),
            vm((FP, 2 * TOK), F32),
            vm((FP, 2 * TOK), BF),
            vm((2, HEADS, 1, TOK), F32),
            vm((2, HEADS, LANES, TOK), BF),
            vm((NY, COLS_IP, FP), BF),
            vm((NY, COLS_IP, FP), BF),
            vm((NY, COLS_IP, FP), F32),
            vm((NY, COLS_IP, FP), BF),
            vm((4, COLS_IP, FP), BF),
            vm((2, COLS_IP, FP), BF),
            vm((3, COLS_IP, FP), BF),
            vm((LANES, FP), BF),
            vm((LANES, LANES), BF),
            vm((NT, ROWS_TP, LANES), BF),
            vm((NT - 1, ROWS_TP, LANES), BF),
            vm((HALF, LANES), BF),
            vm((HALF, LANES), BF),
            vm((HALF, LANES), BF),
            vm((NY - 1, COLS_IP, LANES), BF),
            vm((2 * TOK, DW), BF),
            vm((2, F, TOK), BF),
            vm((2, F, TOK), BF),
            vm((2, F, TOK), BF),
            vm((ROWS_T, COLS_I), BF),
            vm((DW,), F32),
            vm((2, 1, DW), F32),
            dma((NT - 1,)), dma((NT - 1,)),
            dma((8,)), dma((8,)),
            dma((NY,)), dma((NY,)),
            dma((2, 2, 20)), dma((2, 2, 20)),
            dma((NY,)), dma((NY,)),
            dma((16,)), dma((16,)),
            dma((NT - 1,)), dma((NT - 1,)),
            dma((NY,)), dma((NY,)), dma((7,)),
        ],
        compiler_params=pltpu.CompilerParams(
            collective_id=0, has_side_effects=True, vmem_limit_bytes=52 * 2**20
        ),
    )(
        turned(query_in),
        turned(key_in),
        turned(value_in),
        cotangent.reshape(2 * TOK, DW),
        out_weight,
        gate_table,
        time_gate,
    )
    back = lambda a: jnp.swapaxes(a.reshape(2, 1, F, TOK), 2, 3)
    return back(out[0]), back(out[1]), back(out[2]), out[4].reshape(COLS_I), out[3]


def solution(mesh):
    big = P(None, "img", "tok", None)
    return jax.shard_map(
        on_device,
        mesh=mesh,
        in_specs=(big, big, big, big, P("tok", "img"), P(), P(None, "img", None)),
        out_specs=(big, big, big, P("img"), P("tok", "img")),
        check_vma=False,
    )
```
